256 devices in a mesh: row: 8 (over z_lo, core), col: 32 (over z_hi, x, y).
Axes of the slice: x: 4, y: 4, z: 8 (z_hi: 2, z_lo: 4; z = z_hi * 4 + z_lo), core: 2. Of those that a mesh axis runs over, the one named last changes fastest.
Arguments:
- object_field: float32 [2, 2048, 8192], P(None, 'row', 'col'), may hold values from -6 to 6
- probe: float32 [4, 2, 128, 128], replicated, may hold values from -4 to 4
- offsets: int32 [2048, 2], P(('row', 'col')), may hold values from 0 to 255, as said below
- counts: int32 [256], P(('row', 'col')), may hold values from 4 to 8, as said below
- amplitudes: float32 [2048, 128, 128], P(('row', 'col')), may hold values from 0.1 to 3
Outputs:
- new_object: float32 [2, 2048, 8192], P(None, 'row', 'col')
- probe_direction: float32 [4, 2, 128, 128], replicated
The draws below stay inside these ranges and needn't reach their ends.
Inputs may be any that keep to these rules, and one draw needn't show every extreme that they name: Every pattern window lies inside the object: in the last tile row offsets[g,0] <= 128, in the last tile column offsets[g,1] <= 128; elsewhere a window may reach into the tiles below and to the right. Offsets are below their tile's side. `counts`: some tile has all 8 slots live.
All inputs are finite; a program needn't handle non-finite values.
Results may differ from the reference program's by a relative error of at most 0.0003.
Values sent between devices are 32-bit elements; how exact they have to be, the bound alone decides.
A program may use at most 128 MiB of HBM per device.

```python
import math
import jax
import jax.numpy as jnp
from jax import lax

TILE_R = 256
TILE_C = 256
WIN = 128
MODES = 4
SLOTS = 8
NR = 2048
NC = 8192
POSITIONS = 2048
N_ROW = 8
N_COL = 32


def draw_offsets(key, part):
    key = jax.random.fold_in(key, 11)
    total = N_ROW * N_COL * SLOTS
    slot = jnp.arange(total, dtype=jnp.int32)
    tile = slot // SLOTS
    last_row = tile // N_COL == N_ROW - 1
    last_col = tile % N_COL == N_COL - 1
    upper_y = jnp.where(last_row, TILE_R - WIN + 1, TILE_R)
    upper_x = jnp.where(last_col, TILE_C - WIN + 1, TILE_C)
    key_y, key_x = jax.random.split(key)
    rows = jax.random.randint(key_y, (total,), 0, upper_y)
    cols = jax.random.randint(key_x, (total,), 0, upper_x)
    rows = rows.at[0].set(TILE_R - 1).at[1].set(0)
    cols = cols.at[0].set(TILE_C - 1).at[1].set(0)
    return jnp.stack([rows, cols], axis=1).astype(jnp.int32)


def draw_counts(key, part):
    key = jax.random.fold_in(key, 12)
    key_a, key_b = jax.random.split(key)
    tiles = N_ROW * N_COL
    base = jax.random.randint(key_a, (tiles,), SLOTS // 2, SLOTS + 1)
    chosen = jax.random.randint(key_b, (), 0, tiles)
    return base.at[chosen].set(SLOTS).astype(jnp.int32)


def steps_of(rng, dims, cuts, least, high):
    factor_of, own = 1.0, jax.random.fold_in(rng, 6)
    for axis_at, parts in cuts:
        draws = jnp.exp(jax.random.uniform(jax.random.fold_in(own, axis_at), (parts,), jnp.float32, least / len(cuts), high / len(cuts)))
        factor_of = factor_of * jnp.repeat(draws, dims[axis_at] // parts).reshape([-1 if axis == axis_at else 1 for axis in range(len(dims))])
    return factor_of


def gaussian(own_key, shape, deviation, limit, cuts=(), held_as=jnp.bfloat16):
    drawn = deviation * jax.random.normal(own_key, shape, jnp.float32)
    if cuts:
        drawn = drawn * steps_of(own_key, shape, cuts, -0.22, 0.18)
    return jnp.clip(drawn, -limit, limit).astype(held_as)


def setup_inputs(seed: int = 0) -> dict:
    streams_of = jax.random.split(jax.random.key(seed), 6)
    object_field = gaussian(streams_of[0], (2, NR, NC), 1.0, 6.0, ((1, 8), (2, 32)), jnp.float32)
    probe = gaussian(streams_of[1], (MODES, 2, WIN, WIN), 0.5, 4.0, (), jnp.float32)
    offsets = draw_offsets(jax.random.fold_in(streams_of[5], 71), 0)
    counts = draw_counts(jax.random.fold_in(streams_of[5], 71), 0)
    amplitudes = jnp.clip(jnp.exp(math.log(3.0) - 3.4011974 * jax.random.uniform(streams_of[4], (POSITIONS, WIN, WIN), jnp.float32) ** steps_of(streams_of[4], (POSITIONS, WIN, WIN), ((0, 256),), -0.2, 0.2)), 0.1, 3.0)
    return {"object_field": object_field, "probe": probe, "offsets": offsets, "counts": counts, "amplitudes": amplitudes}


HIGH = lax.Precision.HIGHEST

def tables():
    index = jnp.arange(WIN, dtype=jnp.int32)
    phase = (index[:, None] * index[None, :] % WIN).astype(jnp.float32)
    angle = phase * (2.0 * 3.141592653589793 / WIN)
    scale = 1.0 / jnp.sqrt(jnp.float32(WIN))
    return (jnp.cos(angle) * scale, jnp.sin(angle) * scale)

def transform(real, imag, cosine, sine, sign):
    right_re = jnp.einsum('mab,bc->mac', real, cosine, precision=HIGH) + sign * jnp.einsum('mab,bc->mac', imag, sine, precision=HIGH)
    right_im = jnp.einsum('mab,bc->mac', imag, cosine, precision=HIGH) - sign * jnp.einsum('mab,bc->mac', real, sine, precision=HIGH)
    out_re = jnp.einsum('ab,mbc->mac', cosine, right_re, precision=HIGH) + sign * jnp.einsum('ab,mbc->mac', sine, right_im, precision=HIGH)
    out_im = jnp.einsum('ab,mbc->mac', cosine, right_im, precision=HIGH) - sign * jnp.einsum('ab,mbc->mac', sine, right_re, precision=HIGH)
    return (out_re, out_im)

def reference(object_field, probe, offsets, counts, amplitudes):
    cosine, sine = tables()
    pr = probe[:, 0]
    pi = probe[:, 1]
    power = lax.optimization_barrier(jnp.sum(pr * pr + pi * pi, axis=0))
    acc0 = jnp.zeros((3, NR, NC), jnp.float32)
    pnum0 = jnp.zeros((MODES, 2, WIN, WIN), jnp.float32)
    pden0 = jnp.zeros((WIN, WIN), jnp.float32)

    def visit(carry, slot):
        acc, pnum, pden = carry
        tile = slot // SLOTS
        live = (slot % SLOTS < counts[tile]).astype(jnp.float32)
        top = (tile // N_COL * TILE_R + offsets[slot, 0]).astype(jnp.int32)
        left = (tile % N_COL * TILE_C + offsets[slot, 1]).astype(jnp.int32)
        zero = jnp.zeros((), jnp.int32)
        patch = lax.dynamic_slice(object_field, (zero, top, left), (2, WIN, WIN))
        ore = patch[0]
        oim = patch[1]
        psi_re = pr * ore - pi * oim
        psi_im = pr * oim + pi * ore
        far_re, far_im = transform(psi_re, psi_im, cosine, sine, 1.0)
        inten = lax.optimization_barrier(jnp.sum(far_re * far_re + far_im * far_im, axis=0))
        factor = amplitudes[slot] / jnp.sqrt(jnp.maximum(inten, 0.25))
        back_re, back_im = transform(far_re * factor, far_im * factor, cosine, sine, -1.0)
        chi_re = live * (back_re - psi_re)
        chi_im = live * (back_im - psi_im)
        num_re = lax.optimization_barrier(jnp.sum(pr * chi_re + pi * chi_im, axis=0))
        num_im = lax.optimization_barrier(jnp.sum(pr * chi_im - pi * chi_re, axis=0))
        contrib = jnp.stack([num_re, num_im, live * power])
        window = lax.dynamic_slice(acc, (zero, top, left), (3, WIN, WIN))
        acc = lax.dynamic_update_slice(acc, window + contrib, (zero, top, left))
        grad_re = ore * chi_re + oim * chi_im
        grad_im = ore * chi_im - oim * chi_re
        pnum = pnum + jnp.stack([grad_re, grad_im], axis=1)
        pden = pden + live * (ore * ore + oim * oim)
        return ((acc, pnum, pden), None)
    (acc, pnum, pden), unused = lax.scan(visit, (acc0, pnum0, pden0), jnp.arange(POSITIONS, dtype=jnp.int32))
    new_object = object_field + acc[0:2] / (acc[2] + 1.0)
    probe_direction = pnum / jnp.sqrt(pden + 1.0)
    return (new_object, probe_direction)
```

```python
import functools

import jax
import jax.numpy as jnp
import ml_dtypes
import numpy as np
from jax import lax
from jax.experimental import pallas as pl
from jax.experimental.pallas import tpu as pltpu
from jax.sharding import PartitionSpec as P

BF = jnp.bfloat16
F32 = jnp.float32
W = 128
MESH = pl.DeviceIdType.MESH
HBM = pl.BlockSpec(memory_space=pl.ANY)
VMEM = pl.BlockSpec(memory_space=pltpu.VMEM)
SMEM = pl.BlockSpec(memory_space=pltpu.SMEM)
LIMIT = 56 * 2**20


def tables():
    index = np.arange(W)
    angle = (index[:, None] * index[None, :] % W) * (2 * np.pi / W)
    cosine, sine = np.cos(angle) / np.sqrt(W), np.sin(angle) / np.sqrt(W)

    def split(matrix):
        matrix = matrix.astype(np.float32)
        high = matrix.astype(ml_dtypes.bfloat16)
        return high, (matrix - high.astype(np.float32)).astype(ml_dtypes.bfloat16)

    fwd = split(np.block([[cosine, -sine], [sine, cosine]]))
    inv = split(np.block([[cosine, sine], [-sine, cosine]]))
    return fwd, inv


def position():
    return lax.axis_index("row"), lax.axis_index("col")


def count(*flags):
    return sum(flag.astype(jnp.int32) for flag in flags)


PLANE = 16
HALO_RELAYS = (12, 4, 1, 3, 15, 5, 13, 7)
SUMS_RELAYS = (0, 12, 13, 14)


def hilo(x):
    high = x.astype(BF)
    return high, (x - high.astype(F32)).astype(BF)


def dot(a, b):
    return jnp.dot(a, b, preferred_element_type=F32)


def columns(parts):
    return jnp.concatenate(parts, axis=1)


def rows_of(parts):
    return jnp.concatenate(parts, axis=0)


def times_right(high, low, table):
    out = dot(columns([high, low, high]), table[...])
    return [(out[k * W : (k + 1) * W, :W], out[k * W : (k + 1) * W, W:]) for k in range(2)]


def times_left(pairs, table):
    high, low = hilo(columns([rows_of(pair) for pair in pairs]))
    out = dot(table[...], high)
    out = out[: 2 * W] + out[2 * W :] + dot(table[: 2 * W], low)
    return [(out[:W, k * W : (k + 1) * W], out[W:, k * W : (k + 1) * W]) for k in range(2)]


def forward(s, place, ext, probe, amps, table_right, table_left, patch, psi, far_high, far_low, sums):
    top, left, live = place
    block, lanes = left // W, left % W
    lane = lax.broadcasted_iota(jnp.int32, (W, W), 1)
    kept = lane < live * W

    def cut(plane):
        first = ext[plane, block, pl.ds(top, W), :]
        second = ext[plane, block + 1, pl.ds(top, W), :]
        turned = pltpu.roll(jnp.where(lane >= lanes, first, second), (W - lanes) % W, 1)
        return jnp.where(kept, turned, 0.0)

    ore, oim = cut(0), cut(1)
    patch[s, 0], patch[s, 1] = ore, oim
    add_plane(sums, 8, ore * ore + oim * oim)
    inten = jnp.zeros((W, W), F32)
    far = []
    for g in range(0, probe.shape[0], 2):
        for m in (g, g + 1):
            psi[s, m, 0] = probe[m, 0] * ore - probe[m, 1] * oim
            psi[s, m, 1] = probe[m, 0] * oim + probe[m, 1] * ore
        high, low = hilo(rows_of([columns([psi[s, m, 0], psi[s, m, 1]]) for m in (g, g + 1)]))
        pairs = times_left(times_right(high, low, table_right), table_left)
        for real, imag in pairs:
            inten = inten + (real * real + imag * imag)
        far += pairs
    factor = amps[s] * lax.rsqrt(jnp.maximum(inten, 0.25))
    for m, (real, imag) in enumerate(far):
        far_high[s, m], far_low[s, m] = hilo(columns([real * factor, imag * factor]))


def backward(s, probe, table_right, table_left, patch, psi, far_high, far_low, sums):
    num_re, num_im = jnp.zeros((W, W), F32), jnp.zeros((W, W), F32)
    for g in range(0, probe.shape[0], 2):
        high, low = rows_of([far_high[s, g], far_high[s, g + 1]]), rows_of([far_low[s, g], far_low[s, g + 1]])
        pairs = times_left(times_right(high, low, table_right), table_left)
        for m, (real, imag) in zip((g, g + 1), pairs):
            chi_re, chi_im = real - psi[s, m, 0], imag - psi[s, m, 1]
            num_re = num_re + (probe[m, 0] * chi_re + probe[m, 1] * chi_im)
            num_im = num_im + (probe[m, 0] * chi_im - probe[m, 1] * chi_re)
            add_plane(sums, 2 * m, patch[s, 0] * chi_re + patch[s, 1] * chi_im)
            add_plane(sums, 2 * m + 1, patch[s, 0] * chi_im - patch[s, 1] * chi_re)
    return num_re, num_im


DEPTH = 8
UNIT = W // 8
TILES = 10 * UNIT
HALF = TILES // 2
SHARE = HALF // PLANE


def add_plane(sums, plane, value):
    here = pl.ds(plane * UNIT, UNIT)
    sums[here] += value.reshape(UNIT, 8, W)


def placed(shifted, plane, place, count, acc, target):
    lane = lax.broadcasted_iota(jnp.int32, (W, W), 1)
    for part in range(3):

        def add(s, blocks):
            top, left, live = place(s)
            value = shifted[s, plane, pl.ds(2 * W + part * W - top, W), :]
            out = []
            for j, block in enumerate(blocks):
                at = lane + (j * W - left)
                inside = jnp.logical_and(at >= 0, at < live * W)
                out.append(block + jnp.where(inside, value, 0.0))
            return tuple(out)

        blocks = lax.fori_loop(0, count, add, tuple(jnp.zeros((W, W), F32) for _ in range(3)), unroll=True)
        for j in range(3):
            acc[target, j, pl.ds(part * W, W), :] = blocks[j]


def step_kernel(rows, cols, offsets_hbm, counts_hbm, *refs):
    (obj, *hbm), (updated, direction) = refs[:7], refs[7:9]
    (offsets, counts, patch, psi, far_high, far_low, shifted, acc, sums, got, gathered, shard, layers, total) = refs[9:23]
    (from_left, from_above, from_corner, from_high, relay, halo_relay) = refs[23:29]
    (load, halo_send, halo_recv, send, recv, ar_send, ar_recv, ext, *vmem) = refs[29:]
    probe, amps, right_fwd, right_inv, left_fwd, left_inv = vmem
    slot_count = amps.shape[0]
    r, c = position()
    core, z_lo = lax.rem(r, 2), r // 2
    z_hi, xy = c // PLANE, lax.rem(c, PLANE)
    z = z_hi * (DEPTH // 2) + z_lo
    left, up = c > 0, r > 0
    right, down = c < cols - 1, r < rows - 1
    up_left, down_right = jnp.logical_and(up, left), jnp.logical_and(down, right)
    near_right, near_left = jnp.logical_and(right, c != PLANE - 1), jnp.logical_and(left, c != PLANE)
    up_right, turning = jnp.logical_and(up, near_right), jnp.logical_and(down, near_right)
    source, target = c == PLANE - 1, c == PLANE
    target_up = jnp.logical_and(target, up)
    passing = [c == spot for spot in SUMS_RELAYS]
    passing = passing[:2] + [jnp.logical_and(flag, down) for flag in passing[2:]]
    sourced = [source] * 2 + [jnp.logical_and(source, down)] * 2
    east, south, southeast = (r, c + 1), (r + 1, c), (r + 1, c + 1)
    twin = (r + 1 - 2 * core, c)

    def in_plane(k):
        other = lax.rem(xy + k, PLANE)
        return other, (r, z_hi * PLANE + other)

    def in_depth(k):
        other = lax.rem(z + k, DEPTH)
        half = DEPTH // 2
        return lax.rem(other, half) * 2 + core, (other // half) * PLANE + xy

    pieces = [(obj.at[:, :, pl.ds(k * W, W)], ext.at[:, k, pl.ds(0, 2 * W)]) for k in range(2)]
    pieces += [(offsets_hbm, offsets), (counts_hbm, counts)]
    pieces += list(zip(hbm, vmem))
    copies = [pltpu.make_async_copy(src, dst, load.at[k]) for k, (src, dst) in enumerate(pieces)]
    for copy in copies:
        copy.start()

    barrier = pltpu.get_barrier_semaphore()
    peers = [twin] + [in_plane(k)[1] for k in range(1, PLANE)] + [in_depth(k) for k in range(1, DEPTH)]
    ahead = [c == PLANE + spot for spot in HALO_RELAYS]
    ahead_up = [jnp.logical_and(flag, up) for flag in ahead]
    target_down = jnp.logical_and(source, down)
    greetings = [(source, (r, PLANE + spot)) for spot in HALO_RELAYS]
    greetings += [(target_down, (r + 1, PLANE + spot)) for spot in HALO_RELAYS]
    greetings += [(flag, (r, PLANE)) for flag in ahead] + [(near_right, east), (down, south)]
    waits = [near_left, up, *[target for _ in HALO_RELAYS], *ahead, *ahead_up]
    greetings += [(left, (r, c - 1)), (up, (r - 1, c)), (up_left, (r - 1, c - 1))]
    greetings += [(target, (r, spot)) for spot in SUMS_RELAYS[:2]]
    greetings += [(target_up, (r - 1, spot)) for spot in SUMS_RELAYS[2:]]
    greetings += [(flag, (r, PLANE - 1)) for flag in passing]
    for when, device in greetings:

        @pl.when(when)
        def _():
            pl.semaphore_signal(barrier, inc=1, device_id=device, device_id_type=MESH)

    for device in peers:
        pl.semaphore_signal(barrier, inc=1, device_id=device, device_id_type=MESH)
    waits += [right, down, down_right, *sourced, *passing]

    def place(s):
        return offsets[0, s], offsets[1, s], (s < counts[0, 0]).astype(jnp.int32)

    def remote(k, src, dst, device):
        return pltpu.make_async_remote_copy(src, dst, send.at[k], recv.at[k], device_id=device, device_id_type=MESH)

    def summed(k, src, dst, device):
        return pltpu.make_async_remote_copy(src, dst, ar_send.at[k], ar_recv.at[k], device_id=device, device_id_type=MESH)

    def halo(k, src, dst, device):
        return pltpu.make_async_remote_copy(
            src, dst, halo_send.at[k], halo_recv.at[k], device_id=device, device_id_type=MESH
        )

    upper, lower, under_rows = pl.ds(0, W), pl.ds(W, W), pl.ds(2 * W, W)
    west, north = (r, c - 1), (r - 1, c)
    exchange = [
        (near_left, near_right, halo(0, ext.at[:, 0, upper], ext.at[:, 2, upper], west)),
        (up, down, halo(1, ext.at[:, 0, upper], ext.at[:, 0, under_rows], north)),
        (up, down, halo(2, ext.at[:, 1, upper], ext.at[:, 1, under_rows], north)),
        (near_left, near_right, halo(3, ext.at[:, 0, lower], ext.at[:, 2, lower], west)),
    ]
    handed = halo(4, ext.at[:, 2, upper], ext.at[:, 2, under_rows], north)
    relays = len(HALO_RELAYS)
    share = 2 * W // relays
    there, back, above = [], [], []
    for half in range(2):
        for i, spot in enumerate(HALO_RELAYS):
            plane, start = i % 2, i // 2 * share
            span, k = pl.ds(half * W + start, share), 5 + half * relays + i
            held = halo_relay.at[half]
            there.append((target, ahead[i], halo(k, ext.at[plane, 0, span], held, (r, PLANE + spot))))
            back.append((ahead[i], source, halo(k + 2 * relays, held, ext.at[plane, 2, span], (r, PLANE - 1))))
            if half == 0:
                corner_rows = ext.at[plane, 2, pl.ds(2 * W + start, share)]
                above.append((ahead_up[i], target_down, halo(k + 4 * relays, held, corner_rows, (r - 1, PLANE - 1))))
    for copy in copies[:2]:
        copy.wait()
    pl.semaphore_wait(barrier, len(peers) + count(*waits))
    for sends, _, copy in there + exchange:
        pl.when(sends)(copy.start)

    shifted[...] = jnp.zeros_like(shifted)
    sums[...] = jnp.zeros_like(sums)
    for copy in copies[2:]:
        copy.wait()

    power = jnp.zeros((W, W), F32)
    for m in range(probe.shape[0]):
        power = power + (probe[m, 0] * probe[m, 0] + probe[m, 1] * probe[m, 1])

    def weigh(s, carry):
        shifted[s, 2, pl.ds(2 * W, W), :] = pltpu.roll(power, place(s)[1] % W, 1)
        return carry

    lax.fori_loop(0, slot_count, weigh, 0, unroll=True)
    placed(shifted, 2, place, slot_count, acc, 2)
    strip, under, corner = acc.at[:, 2, pl.ds(0, 2 * W)], acc.at[:, pl.ds(0, 2), pl.ds(2 * W, W)], acc.at[:, 2, pl.ds(2 * W, W)]
    weights = [
        (right, left, remote(0, strip.at[2], from_left.at[2], east)),
        (down, up, remote(1, under.at[2], from_above.at[2], south)),
        (down_right, up_left, remote(2, corner.at[2], from_corner.at[2], southeast)),
    ]
    for sends, _, copy in weights:
        pl.when(sends)(copy.start)

    for (_, flag, arriving), (_, _, leaving) in zip(there, back):

        @pl.when(flag)
        def _():
            arriving.wait_recv()
            leaving.start()

    for flag, _, copy in above:
        pl.when(flag)(copy.start)
    pl.when(near_right)(exchange[0][2].wait_recv)
    pl.when(up_right)(handed.start)
    for _, receives, copy in exchange[1:] + back + above + [(up_right, turning, handed)]:
        pl.when(receives)(copy.wait_recv)

    def first(s, carry):
        forward(s, place(s), ext, probe, amps, right_fwd, left_fwd, patch, psi, far_high, far_low, sums)
        return carry

    lax.fori_loop(0, slot_count, first, 0, unroll=True)

    def second(s, carry):
        turn = place(s)[1] % W
        for plane, value in enumerate(backward(s, probe, right_inv, left_inv, patch, psi, far_high, far_low, sums)):
            shifted[s, plane, pl.ds(2 * W, W), :] = pltpu.roll(value, turn, 1)
        return carry

    lax.fori_loop(0, slot_count, second, 0, unroll=True)

    mine = pl.ds(core * HALF, HALF)
    swap = summed(0, sums.at[pl.ds((1 - core) * HALF, HALF)], got, twin)
    swap.start()
    placed(shifted, 0, place, slot_count, acc, 0)
    swap.wait_recv()
    got[...] += sums[mine]

    scatter = []
    for k in range(1, PLANE):
        other, device = in_plane(k)
        scatter.append(summed(k, got.at[pl.ds(other * SHARE, SHARE)], gathered.at[k - 1], device))
        scatter[-1].start()
    placed(shifted, 1, place, slot_count, acc, 1)
    numer = pl.ds(0, 2)
    crossing = [(strip.at[p, lower], from_left.at[p, lower], (r, PLANE)) for p in range(2)]
    crossing += [(corner.at[p], from_corner.at[p], (r + 1, PLANE)) for p in range(2)]
    pass_on = [remote(3 + i, src, relay, (r, spot)) for i, ((src, _, _), spot) in enumerate(zip(crossing, SUMS_RELAYS))]
    passed = [remote(7 + i, relay, dst, device) for i, (_, dst, device) in enumerate(crossing)]
    turned = remote(11, corner.at[numer], from_high, south)
    plan = [
        (turning, up_right, turned),
        (near_right, near_left, remote(12, strip.at[numer, lower], from_left.at[numer, lower], east)),
        (down, up, remote(13, under.at[numer], from_above.at[numer], south)),
    ]
    late = remote(14, strip.at[numer, upper], from_left.at[numer, upper], east)
    for flag, copy in zip(sourced, pass_on):
        pl.when(flag)(copy.start)
    pl.when(source)(late.start)
    for sends, _, copy in plan:
        pl.when(sends)(copy.start)
    value = got[pl.ds(xy * SHARE, SHARE)]
    for k in range(1, PLANE):
        scatter[k - 1].wait_recv()
        value = value + gathered[k - 1]
    shard[...] = value

    spread = []
    for k in range(1, DEPTH):
        spread.append(summed(PLANE - 1 + k, shard, layers.at[z], in_depth(k)))
        spread[-1].start()
    layers[z] = value
    for flag, arriving, leaving in zip(passing, pass_on, passed):

        @pl.when(flag)
        def _():
            arriving.wait_recv()
            leaving.start()

    @pl.when(up_right)
    def _():
        turned.wait_recv()
        strip[numer, upper] += from_high[...]

    pl.when(near_right)(late.start)
    for copy in spread:
        copy.wait_recv()
    value = layers[0]
    for k in range(1, DEPTH):
        value = value + layers[k]
    here = pl.ds(core * HALF + xy * SHARE, SHARE)
    total[here] = value

    gather = []
    for k in range(1, PLANE):
        gather.append(summed(PLANE + DEPTH - 2 + k, total.at[here], total.at[here], in_plane(k)[1]))
        gather[-1].start()

    for copy in gather:
        copy.wait_recv()
    half = total.at[mine]
    last = summed(2 * PLANE + DEPTH - 2, half, half, twin)
    last.start()

    for _, receives, copy in weights + plan[1:]:
        pl.when(receives)(copy.wait_recv)
    for flag, copy in zip([target] * 2 + [target_up] * 2, passed):
        pl.when(flag)(copy.wait_recv)
    pl.when(left)(late.wait_recv)

    def taken(flag, value):
        return jnp.where(jnp.broadcast_to(flag.astype(jnp.int32), value.shape) > 0, value, 0.0)

    for i in range(2):
        for j in range(2):
            span = pl.ds(i * W, W)
            parts = []
            for plane in range(3):
                value = acc[plane, j, span, :]
                if j == 0:
                    value = value + taken(left, from_left[plane, span, :])
                if i == 0:
                    value = value + taken(up, from_above[plane, j])
                if i == 0 and j == 0:
                    value = value + taken(up_left if plane == 2 else target_up, from_corner[plane])
                parts.append(value)
            scale = 1.0 / (parts[2] + 1.0)
            for plane in range(2):
                updated[plane, span, pl.ds(j * W, W)] = ext[plane, j, span, :] + parts[plane] * scale

    last.wait_recv()
    scale = lax.rsqrt(total[pl.ds(8 * UNIT, UNIT)] + 1.0)
    for plane in range(8):
        direction[plane] = total[pl.ds(plane * UNIT, UNIT)] * scale
    for copy in [swap, *scatter, *spread, *gather, last]:
        copy.wait_send()
    for sends, _, copy in exchange + there + back + above + [(up_right, turning, handed)] + weights + plan:
        pl.when(sends)(copy.wait_send)
    for flag, copy in zip(sourced + passing, pass_on + passed):
        pl.when(flag)(copy.wait_send)
    pl.when(right)(late.wait_send)


def step(obj, probe, offsets, counts, amps, rows, cols):
    fwd, inv = tables()
    consts = [
        np.concatenate([fwd[0], fwd[0], fwd[1]], 0),
        np.concatenate([inv[0], inv[0], inv[1]], 0),
        np.concatenate([inv[0], inv[1]], 0),
        np.concatenate([fwd[0], fwd[1]], 0),
    ]
    loaded = [probe, amps] + [jnp.asarray(v) for v in consts]
    slot_count, modes = amps.shape[0], probe.shape[0]
    dma = pltpu.SemaphoreType.DMA
    messages = 2 * PLANE + DEPTH - 1
    return pl.pallas_call(
        functools.partial(step_kernel, rows, cols),
        out_shape=(
            pltpu.VMEM(obj.shape, F32),
            pltpu.VMEM((8, UNIT, 8, W), F32),
        ),
        in_specs=[HBM] * 9,
        out_specs=(VMEM, VMEM),
        scratch_shapes=[
            pltpu.SMEM(offsets.shape[::-1], jnp.int32),
            pltpu.SMEM((1, 1), jnp.int32),
            pltpu.VMEM((slot_count, 2, W, W), F32),
            pltpu.VMEM((slot_count, modes, 2, W, W), F32),
            pltpu.VMEM((slot_count, modes, W, 2 * W), BF),
            pltpu.VMEM((slot_count, modes, W, 2 * W), BF),
            pltpu.VMEM((slot_count, 3, 5 * W, W), F32),
            pltpu.VMEM((3, 3, 3 * W, W), F32),
            pltpu.VMEM((TILES, 8, W), F32),
            pltpu.VMEM((HALF, 8, W), F32),
            pltpu.VMEM((PLANE - 1, SHARE, 8, W), F32),
            pltpu.VMEM((SHARE, 8, W), F32),
            pltpu.VMEM((DEPTH, SHARE, 8, W), F32),
            pltpu.VMEM((TILES, 8, W), F32),
            pltpu.VMEM((3, 2 * W, W), F32),
            pltpu.VMEM((3, 2, W, W), F32),
            pltpu.VMEM((3, W, W), F32),
            pltpu.VMEM((2, W, W), F32),
            pltpu.VMEM((W, W), F32),
            pltpu.VMEM((2, 2 * W // len(HALO_RELAYS), W), F32),
            dma((10,)),
            dma((5 + 5 * len(HALO_RELAYS),)),
            dma((5 + 5 * len(HALO_RELAYS),)),
            dma((15,)),
            dma((15,)),
            dma((messages,)),
            dma((messages,)),
            pltpu.VMEM((2, 3, 3 * W, W), F32),
        ]
        + [pltpu.VMEM(v.shape, v.dtype) for v in loaded],
        compiler_params=pltpu.CompilerParams(collective_id=0, has_side_effects=True, vmem_limit_bytes=LIMIT),
        name="step",
    )(offsets.T, counts[None], obj, *loaded)


def body(rows, cols, object_field, probe, offsets, counts, amplitudes):
    new_object, direction = step(object_field, probe, offsets, counts, amplitudes, rows, cols)
    return new_object, direction.reshape(probe.shape)


def solution(mesh):
    rows, cols = mesh.shape["row"], mesh.shape["col"]
    return jax.shard_map(
        functools.partial(body, rows, cols),
        mesh=mesh,
        in_specs=(
            P(None, "row", "col"),
            P(),
            P(("row", "col"), None),
            P(("row", "col")),
            P(("row", "col"), None, None),
        ),
        out_specs=(P(None, "row", "col"), P()),
        check_vma=False,
    )
```

```python
import functools

import jax
import jax.numpy as jnp
import ml_dtypes
import numpy as np
from jax import lax
from jax.experimental import pallas as pl
from jax.experimental.pallas import tpu as pltpu
from jax.sharding import PartitionSpec as P

BF = jnp.bfloat16
F32 = jnp.float32
W = 128
MESH = pl.DeviceIdType.MESH
HBM = pl.BlockSpec(memory_space=pl.ANY)
VMEM = pl.BlockSpec(memory_space=pltpu.VMEM)
SMEM = pl.BlockSpec(memory_space=pltpu.SMEM)
LIMIT = 56 * 2**20


def tables():
    index = np.arange(W)
    angle = (index[:, None] * index[None, :] % W) * (2 * np.pi / W)
    cosine, sine = np.cos(angle) / np.sqrt(W), np.sin(angle) / np.sqrt(W)

    def split(matrix):
        matrix = matrix.astype(np.float32)
        high = matrix.astype(ml_dtypes.bfloat16)
        return high, (matrix - high.astype(np.float32)).astype(ml_dtypes.bfloat16)

    fwd = split(np.block([[cosine, -sine], [sine, cosine]]))
    inv = split(np.block([[cosine, sine], [-sine, cosine]]))
    return fwd, inv


def position():
    return lax.axis_index("row"), lax.axis_index("col")


def count(*flags):
    return sum(flag.astype(jnp.int32) for flag in flags)


PLANE = 16
HALO_RELAYS = (12, 4, 1, 3, 15, 5, 13, 7)
SUMS_RELAYS = (0, 12, 13, 14)


def hilo(x):
    high = x.astype(BF)
    return high, (x - high.astype(F32)).astype(BF)


def dot(a, b):
    return jnp.dot(a, b, preferred_element_type=F32)


def columns(parts):
    return jnp.concatenate(parts, axis=1)


def rows_of(parts):
    return jnp.concatenate(parts, axis=0)


def times_right(high, low, table):
    out = dot(columns([high, low, high]), table[...])
    return [(out[k * W : (k + 1) * W, :W], out[k * W : (k + 1) * W, W:]) for k in range(2)]


def times_left(pairs, table):
    high, low = hilo(columns([rows_of(pair) for pair in pairs]))
    out = dot(table[...], high)
    out = out[: 2 * W] + out[2 * W :] + dot(table[: 2 * W], low)
    return [(out[:W, k * W : (k + 1) * W], out[W:, k * W : (k + 1) * W]) for k in range(2)]


def forward(s, place, ext, probe, amps, table_right, table_left, patch, psi, far_high, far_low, sums):
    top, left, live = place
    block, lanes = left // W, left % W
    lane = lax.broadcasted_iota(jnp.int32, (W, W), 1)
    kept = lane < live * W

    def cut(plane):
        first = ext[plane, block, pl.ds(top, W), :]
        second = ext[plane, block + 1, pl.ds(top, W), :]
        turned = pltpu.roll(jnp.where(lane >= lanes, first, second), (W - lanes) % W, 1)
        return jnp.where(kept, turned, 0.0)

    ore, oim = cut(0), cut(1)
    patch[s, 0], patch[s, 1] = ore, oim
    add_plane(sums, 8, ore * ore + oim * oim)
    inten = jnp.zeros((W, W), F32)
    far = []
    for g in range(0, probe.shape[0], 2):
        for m in (g, g + 1):
            psi[s, m, 0] = probe[m, 0] * ore - probe[m, 1] * oim
            psi[s, m, 1] = probe[m, 0] * oim + probe[m, 1] * ore
        high, low = hilo(rows_of([columns([psi[s, m, 0], psi[s, m, 1]]) for m in (g, g + 1)]))
        pairs = times_left(times_right(high, low, table_right), table_left)
        for real, imag in pairs:
            inten = inten + (real * real + imag * imag)
        far += pairs
    factor = amps[s] * lax.rsqrt(jnp.maximum(inten, 0.25))
    for m, (real, imag) in enumerate(far):
        far_high[s, m], far_low[s, m] = hilo(columns([real * factor, imag * factor]))


def backward(s, probe, table_right, table_left, patch, psi, far_high, far_low, sums):
    num_re, num_im = jnp.zeros((W, W), F32), jnp.zeros((W, W), F32)
    for g in range(0, probe.shape[0], 2):
        high, low = rows_of([far_high[s, g], far_high[s, g + 1]]), rows_of([far_low[s, g], far_low[s, g + 1]])
        pairs = times_left(times_right(high, low, table_right), table_left)
        for m, (real, imag) in zip((g, g + 1), pairs):
            chi_re, chi_im = real - psi[s, m, 0], imag - psi[s, m, 1]
            num_re = num_re + (probe[m, 0] * chi_re + probe[m, 1] * chi_im)
            num_im = num_im + (probe[m, 0] * chi_im - probe[m, 1] * chi_re)
            add_plane(sums, 2 * m, patch[s, 0] * chi_re + patch[s, 1] * chi_im)
            add_plane(sums, 2 * m + 1, patch[s, 0] * chi_im - patch[s, 1] * chi_re)
    return num_re, num_im


DEPTH = 8
UNIT = W // 8
TILES = 10 * UNIT
HALF = TILES // 2
SHARE = HALF // PLANE


def add_plane(sums, plane, value):
    here = pl.ds(plane * UNIT, UNIT)
    sums[here] += value.reshape(UNIT, 8, W)


def placed(shifted, plane, place, count, acc, target):
    lane = lax.broadcasted_iota(jnp.int32, (W, W), 1)
    for part in range(3):

        def add(s, blocks):
            top, left, live = place(s)
            value = shifted[s, plane, pl.ds(2 * W + part * W - top, W), :]
            out = []
            for j, block in enumerate(blocks):
                at = lane + (j * W - left)
                inside = jnp.logical_and(at >= 0, at < live * W)
                out.append(block + jnp.where(inside, value, 0.0))
            return tuple(out)

        blocks = lax.fori_loop(0, count, add, tuple(jnp.zeros((W, W), F32) for _ in range(3)), unroll=True)
        for j in range(3):
            acc[target, j, pl.ds(part * W, W), :] = blocks[j]


def step_kernel(rows, cols, offsets_hbm, counts_hbm, *refs):
    (obj, *hbm), (updated, direction) = refs[:7], refs[7:9]
    (offsets, counts, patch, psi, far_high, far_low, shifted, acc, sums, got, gathered, shard, layers, total) = refs[9:23]
    (from_left, from_above, from_corner, from_high, relay, halo_relay) = refs[23:29]
    (load, halo_send, halo_recv, send, recv, ar_send, ar_recv, ext, *vmem) = refs[29:]
    probe, amps, right_fwd, right_inv, left_fwd, left_inv = vmem
    slot_count = amps.shape[0]
    r, c = position()
    core, z_lo = lax.rem(r, 2), r // 2
    z_hi, xy = c // PLANE, lax.rem(c, PLANE)
    z = z_hi * (DEPTH // 2) + z_lo
    left, up = c > 0, r > 0
    right, down = c < cols - 1, r < rows - 1
    up_left, down_right = jnp.logical_and(up, left), jnp.logical_and(down, right)
    near_right, near_left = jnp.logical_and(right, c != PLANE - 1), jnp.logical_and(left, c != PLANE)
    up_right, turning = jnp.logical_and(up, near_right), jnp.logical_and(down, near_right)
    source, target = c == PLANE - 1, c == PLANE
    target_up = jnp.logical_and(target, up)
    passing = [c == spot for spot in SUMS_RELAYS]
    passing = passing[:2] + [jnp.logical_and(flag, down) for flag in passing[2:]]
    sourced = [source] * 2 + [jnp.logical_and(source, down)] * 2
    east, south, southeast = (r, c + 1), (r + 1, c), (r + 1, c + 1)
    twin = (r + 1 - 2 * core, c)

    def in_plane(k):
        other = lax.rem(xy + k, PLANE)
        return other, (r, z_hi * PLANE + other)

    def in_depth(k):
        other = lax.rem(z + k, DEPTH)
        half = DEPTH // 2
        return lax.rem(other, half) * 2 + core, (other // half) * PLANE + xy

    pieces = [(obj.at[:, :, pl.ds(k * W, W)], ext.at[:, k, pl.ds(0, 2 * W)]) for k in range(2)]
    pieces += [(offsets_hbm, offsets), (counts_hbm, counts)]
    pieces += list(zip(hbm, vmem))
    copies = [pltpu.make_async_copy(src, dst, load.at[k]) for k, (src, dst) in enumerate(pieces)]
    for copy in copies:
        copy.start()

    barrier = pltpu.get_barrier_semaphore()
    peers = [twin] + [in_plane(k)[1] for k in range(1, PLANE)] + [in_depth(k) for k in range(1, DEPTH)]
    ahead = [c == PLANE + spot for spot in HALO_RELAYS]
    ahead_up = [jnp.logical_and(flag, up) for flag in ahead]
    target_down = jnp.logical_and(source, down)
    greetings = [(source, (r, PLANE + spot)) for spot in HALO_RELAYS]
    greetings += [(target_down, (r + 1, PLANE + spot)) for spot in HALO_RELAYS]
    greetings += [(flag, (r, PLANE)) for flag in ahead] + [(near_right, east), (down, south)]
    waits = [near_left, up, *[target for _ in HALO_RELAYS], *ahead, *ahead_up]
    greetings += [(left, (r, c - 1)), (up, (r - 1, c)), (up_left, (r - 1, c - 1))]
    greetings += [(target, (r, spot)) for spot in SUMS_RELAYS[:2]]
    greetings += [(target_up, (r - 1, spot)) for spot in SUMS_RELAYS[2:]]
    greetings += [(flag, (r, PLANE - 1)) for flag in passing]
    for when, device in greetings:

        @pl.when(when)
        def _():
            pl.semaphore_signal(barrier, inc=1, device_id=device, device_id_type=MESH)

    for device in peers:
        pl.semaphore_signal(barrier, inc=1, device_id=device, device_id_type=MESH)
    waits += [right, down, down_right, *sourced, *passing]

    def place(s):
        return offsets[0, s], offsets[1, s], (s < counts[0, 0]).astype(jnp.int32)

    def remote(k, j, src, dst, device):
        return pltpu.make_async_remote_copy(src, dst, send.at[k], recv.at[j], device_id=device, device_id_type=MESH)

    def landed(when, ref, semaphore):
        wait = pltpu.make_async_copy(ref, ref, semaphore).wait
        if when is None:
            wait()
        else:
            pl.when(when)(wait)

    def summed(k, src, dst, device):
        return pltpu.make_async_remote_copy(src, dst, ar_send.at[k], ar_recv.at[k], device_id=device, device_id_type=MESH)

    def halo(k, j, src, dst, device):
        return pltpu.make_async_remote_copy(
            src, dst, halo_send.at[k], halo_recv.at[j], device_id=device, device_id_type=MESH
        )

    upper, lower, under_rows = pl.ds(0, W), pl.ds(W, W), pl.ds(2 * W, W)
    west, north = (r, c - 1), (r - 1, c)
    exchange = [
        (near_left, near_right, halo(0, 0, ext.at[:, 0, upper], ext.at[:, 2, upper], west)),
        (up, down, halo(1, 1, ext.at[:, 0, upper], ext.at[:, 0, under_rows], north)),
        (up, down, halo(2, 2, ext.at[:, 1, upper], ext.at[:, 1, under_rows], north)),
        (near_left, near_right, halo(3, 3, ext.at[:, 0, lower], ext.at[:, 2, lower], west)),
    ]
    handed = halo(4, 4, ext.at[:, 2, upper], ext.at[:, 2, under_rows], north)
    relays = len(HALO_RELAYS)
    share = 2 * W // relays
    there, back, above = [], [], []
    for half in range(2):
        for i, spot in enumerate(HALO_RELAYS):
            plane, start = i % 2, i // 2 * share
            span = pl.ds(half * W + start, share)
            held = halo_relay.at[half]
            there.append((target, ahead[i], halo(5, 5 + half, ext.at[plane, 0, span], held, (r, PLANE + spot))))
            back.append((ahead[i], source, halo(6 + half, 7 + half, held, ext.at[plane, 2, span], (r, PLANE - 1))))
            if half == 0:
                corner_rows = ext.at[plane, 2, pl.ds(2 * W + start, share)]
                above.append((ahead_up[i], target_down, halo(8, 9, held, corner_rows, (r - 1, PLANE - 1))))
    for copy in copies[:2]:
        copy.wait()
    pl.semaphore_wait(barrier, len(peers) + count(*waits))
    for sends, _, copy in there + exchange:
        pl.when(sends)(copy.start)

    shifted[...] = jnp.zeros_like(shifted)
    sums[...] = jnp.zeros_like(sums)
    for copy in copies[2:]:
        copy.wait()

    power = jnp.zeros((W, W), F32)
    for m in range(probe.shape[0]):
        power = power + (probe[m, 0] * probe[m, 0] + probe[m, 1] * probe[m, 1])

    def weigh(s, carry):
        shifted[s, 2, pl.ds(2 * W, W), :] = pltpu.roll(power, place(s)[1] % W, 1)
        return carry

    lax.fori_loop(0, slot_count, weigh, 0, unroll=True)
    placed(shifted, 2, place, slot_count, acc, 2)
    strip, under, corner = acc.at[:, 2, pl.ds(0, 2 * W)], acc.at[:, pl.ds(0, 2), pl.ds(2 * W, W)], acc.at[:, 2, pl.ds(2 * W, W)]
    weights = [
        (right, left, remote(0, 0, strip.at[2], from_left.at[2], east)),
        (down, up, remote(1, 1, under.at[2], from_above.at[2], south)),
        (down_right, up_left, remote(2, 2, corner.at[2], from_corner.at[2], southeast)),
    ]
    for sends, _, copy in weights:
        pl.when(sends)(copy.start)

    for (_, flag, arriving), (_, _, leaving) in zip(there, back):

        @pl.when(flag)
        def _():
            arriving.wait_recv()
            leaving.start()

    for flag, _, copy in above:
        pl.when(flag)(copy.start)
    pl.when(near_right)(exchange[0][2].wait_recv)
    pl.when(up_right)(handed.start)
    for _, receives, copy in exchange[1:] + [(up_right, turning, handed)]:
        pl.when(receives)(copy.wait_recv)
    landed(source, ext.at[:, 2, upper], halo_recv.at[7])
    landed(source, ext.at[:, 2, lower], halo_recv.at[8])
    landed(target_down, ext.at[:, 2, under_rows], halo_recv.at[9])

    def first(s, carry):
        forward(s, place(s), ext, probe, amps, right_fwd, left_fwd, patch, psi, far_high, far_low, sums)
        return carry

    lax.fori_loop(0, slot_count, first, 0, unroll=True)

    def second(s, carry):
        turn = place(s)[1] % W
        for plane, value in enumerate(backward(s, probe, right_inv, left_inv, patch, psi, far_high, far_low, sums)):
            shifted[s, plane, pl.ds(2 * W, W), :] = pltpu.roll(value, turn, 1)
        return carry

    lax.fori_loop(0, slot_count, second, 0, unroll=True)

    mine = pl.ds(core * HALF, HALF)
    swap = summed(0, sums.at[pl.ds((1 - core) * HALF, HALF)], got, twin)
    swap.start()
    placed(shifted, 0, place, slot_count, acc, 0)
    swap.wait_recv()
    got[...] += sums[mine]

    for k in range(1, PLANE):
        other, device = in_plane(k)
        summed(1, got.at[pl.ds(other * SHARE, SHARE)], gathered.at[k - 1], device).start()
    placed(shifted, 1, place, slot_count, acc, 1)
    numer = pl.ds(0, 2)
    crossing = [(strip.at[p, lower], from_left.at[p, lower], (r, PLANE)) for p in range(2)]
    crossing += [(corner.at[p], from_corner.at[p], (r + 1, PLANE)) for p in range(2)]
    pass_on = [remote(3 + i, 3, src, relay, (r, spot)) for i, ((src, _, _), spot) in enumerate(zip(crossing, SUMS_RELAYS))]
    passed = [remote(7, 4 + i // 2, relay, dst, device) for i, (_, dst, device) in enumerate(crossing)]
    turned = remote(8, 6, corner.at[numer], from_high, south)
    plan = [
        (turning, up_right, turned),
        (near_right, near_left, remote(9, 7, strip.at[numer, lower], from_left.at[numer, lower], east)),
        (down, up, remote(10, 8, under.at[numer], from_above.at[numer], south)),
    ]
    late = remote(11, 9, strip.at[numer, upper], from_left.at[numer, upper], east)
    for flag, copy in zip(sourced, pass_on):
        pl.when(flag)(copy.start)
    pl.when(source)(late.start)
    for sends, _, copy in plan:
        pl.when(sends)(copy.start)
    value = got[pl.ds(xy * SHARE, SHARE)]
    landed(None, gathered, ar_recv.at[1])
    for k in range(1, PLANE):
        value = value + gathered[k - 1]
    shard[...] = value

    for k in range(1, DEPTH):
        summed(2, shard, layers.at[z], in_depth(k)).start()
    layers[z] = value
    for flag, arriving, leaving in zip(passing, pass_on, passed):

        @pl.when(flag)
        def _():
            arriving.wait_recv()
            leaving.start()

    @pl.when(up_right)
    def _():
        turned.wait_recv()
        strip[numer, upper] += from_high[...]

    pl.when(near_right)(late.start)
    landed(None, layers.at[pl.ds(0, DEPTH - 1)], ar_recv.at[2])
    value = layers[0]
    for k in range(1, DEPTH):
        value = value + layers[k]
    here = pl.ds(core * HALF + xy * SHARE, SHARE)
    total[here] = value

    for k in range(1, PLANE):
        summed(3, total.at[here], total.at[here], in_plane(k)[1]).start()

    others = pl.ds(core * HALF, HALF - SHARE)
    landed(None, total.at[others], ar_recv.at[3])
    half = total.at[mine]
    last = summed(4, half, half, twin)
    last.start()

    for _, receives, copy in weights + plan[1:]:
        pl.when(receives)(copy.wait_recv)
    landed(target, from_left.at[numer, lower], recv.at[4])
    landed(target_up, from_corner.at[numer], recv.at[5])
    pl.when(left)(late.wait_recv)

    def taken(flag, value):
        return jnp.where(jnp.broadcast_to(flag.astype(jnp.int32), value.shape) > 0, value, 0.0)

    for i in range(2):
        for j in range(2):
            span = pl.ds(i * W, W)
            parts = []
            for plane in range(3):
                value = acc[plane, j, span, :]
                if j == 0:
                    value = value + taken(left, from_left[plane, span, :])
                if i == 0:
                    value = value + taken(up, from_above[plane, j])
                if i == 0 and j == 0:
                    value = value + taken(up_left if plane == 2 else target_up, from_corner[plane])
                parts.append(value)
            scale = 1.0 / (parts[2] + 1.0)
            for plane in range(2):
                updated[plane, span, pl.ds(j * W, W)] = ext[plane, j, span, :] + parts[plane] * scale

    last.wait_recv()
    scale = lax.rsqrt(total[pl.ds(8 * UNIT, UNIT)] + 1.0)
    for plane in range(8):
        direction[plane] = total[pl.ds(plane * UNIT, UNIT)] * scale
    for copy in [swap, last]:
        copy.wait_send()
    landed(None, got.at[pl.ds(0, HALF - SHARE)], ar_send.at[1])
    landed(None, layers.at[pl.ds(0, DEPTH - 1)], ar_send.at[2])
    landed(None, total.at[others], ar_send.at[3])
    for sends, _, copy in exchange + back + above + [(up_right, turning, handed)] + weights + plan:
        pl.when(sends)(copy.wait_send)
    landed(target, ext.at[:, 0, pl.ds(0, 2 * W)], halo_send.at[5])
    for flag, copy in zip(sourced + passing, pass_on + passed):
        pl.when(flag)(copy.wait_send)
    pl.when(right)(late.wait_send)


def step(obj, probe, offsets, counts, amps, rows, cols):
    fwd, inv = tables()
    consts = [
        np.concatenate([fwd[0], fwd[0], fwd[1]], 0),
        np.concatenate([inv[0], inv[0], inv[1]], 0),
        np.concatenate([inv[0], inv[1]], 0),
        np.concatenate([fwd[0], fwd[1]], 0),
    ]
    loaded = [probe, amps] + [jnp.asarray(v) for v in consts]
    slot_count, modes = amps.shape[0], probe.shape[0]
    dma = pltpu.SemaphoreType.DMA
    messages = 5
    return pl.pallas_call(
        functools.partial(step_kernel, rows, cols),
        out_shape=(
            pltpu.VMEM(obj.shape, F32),
            pltpu.VMEM((8, UNIT, 8, W), F32),
        ),
        in_specs=[HBM] * 9,
        out_specs=(VMEM, VMEM),
        scratch_shapes=[
            pltpu.SMEM(offsets.shape[::-1], jnp.int32),
            pltpu.SMEM((1, 1), jnp.int32),
            pltpu.VMEM((slot_count, 2, W, W), F32),
            pltpu.VMEM((slot_count, modes, 2, W, W), F32),
            pltpu.VMEM((slot_count, modes, W, 2 * W), BF),
            pltpu.VMEM((slot_count, modes, W, 2 * W), BF),
            pltpu.VMEM((slot_count, 3, 5 * W, W), F32),
            pltpu.VMEM((3, 3, 3 * W, W), F32),
            pltpu.VMEM((TILES, 8, W), F32),
            pltpu.VMEM((HALF, 8, W), F32),
            pltpu.VMEM((PLANE - 1, SHARE, 8, W), F32),
            pltpu.VMEM((SHARE, 8, W), F32),
            pltpu.VMEM((DEPTH, SHARE, 8, W), F32),
            pltpu.VMEM((TILES, 8, W), F32),
            pltpu.VMEM((3, 2 * W, W), F32),
            pltpu.VMEM((3, 2, W, W), F32),
            pltpu.VMEM((3, W, W), F32),
            pltpu.VMEM((2, W, W), F32),
            pltpu.VMEM((W, W), F32),
            pltpu.VMEM((2, 2 * W // len(HALO_RELAYS), W), F32),
            dma((10,)),
            dma((9,)),
            dma((10,)),
            dma((12,)),
            dma((10,)),
            dma((messages,)),
            dma((messages,)),
            pltpu.VMEM((2, 3, 3 * W, W), F32),
        ]
        + [pltpu.VMEM(v.shape, v.dtype) for v in loaded],
        compiler_params=pltpu.CompilerParams(collective_id=0, has_side_effects=True, vmem_limit_bytes=LIMIT),
        name="step",
    )(offsets.T, counts[None], obj, *loaded)


def body(rows, cols, object_field, probe, offsets, counts, amplitudes):
    new_object, direction = step(object_field, probe, offsets, counts, amplitudes, rows, cols)
    return new_object, direction.reshape(probe.shape)


def solution(mesh):
    rows, cols = mesh.shape["row"], mesh.shape["col"]
    return jax.shard_map(
        functools.partial(body, rows, cols),
        mesh=mesh,
        in_specs=(
            P(None, "row", "col"),
            P(),
            P(("row", "col"), None),
            P(("row", "col")),
            P(("row", "col"), None, None),
        ),
        out_specs=(P(None, "row", "col"), P()),
        check_vma=False,
    )
```

```python
import functools

import jax
import jax.numpy as jnp
import ml_dtypes
import numpy as np
from jax import lax
from jax.experimental import pallas as pl
from jax.experimental.pallas import tpu as pltpu
from jax.sharding import PartitionSpec as P

BF = jnp.bfloat16
F32 = jnp.float32
W = 128
MESH = pl.DeviceIdType.MESH
HBM = pl.BlockSpec(memory_space=pl.ANY)
VMEM = pl.BlockSpec(memory_space=pltpu.VMEM)
SMEM = pl.BlockSpec(memory_space=pltpu.SMEM)
LIMIT = 56 * 2**20


def tables():
    index = np.arange(W)
    angle = (index[:, None] * index[None, :] % W) * (2 * np.pi / W)
    cosine, sine = np.cos(angle) / np.sqrt(W), np.sin(angle) / np.sqrt(W)

    def split(matrix):
        matrix = matrix.astype(np.float32)
        high = matrix.astype(ml_dtypes.bfloat16)
        return high, (matrix - high.astype(np.float32)).astype(ml_dtypes.bfloat16)

    fwd = split(np.block([[cosine, -sine], [sine, cosine]]))
    inv = split(np.block([[cosine, sine], [-sine, cosine]]))
    return fwd, inv


def position():
    return lax.axis_index("row"), lax.axis_index("col")


def count(*flags):
    return sum(flag.astype(jnp.int32) for flag in flags)


PLANE = 16
HALO_RELAYS = (12, 4, 1, 3, 15, 5, 13, 7)
SUMS_RELAYS = (0, 12, 13, 14)


def hilo(x):
    high = x.astype(BF)
    return high, (x - high.astype(F32)).astype(BF)


def dot(a, b):
    return jnp.dot(a, b, preferred_element_type=F32)


def columns(parts):
    return jnp.concatenate(parts, axis=1)


def rows_of(parts):
    return jnp.concatenate(parts, axis=0)


def times_right(high, low, table):
    out = dot(columns([high, low, high]), table[...])
    return [(out[k * W : (k + 1) * W, :W], out[k * W : (k + 1) * W, W:]) for k in range(2)]


def times_left(pairs, table):
    high, low = hilo(columns([rows_of(pair) for pair in pairs]))
    out = dot(table[...], high)
    out = out[: 2 * W] + out[2 * W :] + dot(table[: 2 * W], low)
    return [(out[:W, k * W : (k + 1) * W], out[W:, k * W : (k + 1) * W]) for k in range(2)]


def forward(s, place, ext, probe, amps, table_right, table_left, patch, psi, far_high, far_low, sums):
    top, left, live = place
    block, lanes = left // W, left % W
    lane = lax.broadcasted_iota(jnp.int32, (W, W), 1)
    kept = lane < live * W

    def cut(plane):
        first = ext[plane, block, pl.ds(top, W), :]
        second = ext[plane, block + 1, pl.ds(top, W), :]
        turned = pltpu.roll(jnp.where(lane >= lanes, first, second), (W - lanes) % W, 1)
        return jnp.where(kept, turned, 0.0)

    ore, oim = cut(0), cut(1)
    patch[s, 0], patch[s, 1] = ore, oim
    add_plane(sums, 8, ore * ore + oim * oim)
    inten = jnp.zeros((W, W), F32)
    far = []
    for g in range(0, probe.shape[0], 2):
        for m in (g, g + 1):
            psi[s, m, 0] = probe[m, 0] * ore - probe[m, 1] * oim
            psi[s, m, 1] = probe[m, 0] * oim + probe[m, 1] * ore
        high, low = hilo(rows_of([columns([psi[s, m, 0], psi[s, m, 1]]) for m in (g, g + 1)]))
        pairs = times_left(times_right(high, low, table_right), table_left)
        for real, imag in pairs:
            inten = inten + (real * real + imag * imag)
        far += pairs
    factor = amps[s] * lax.rsqrt(jnp.maximum(inten, 0.25))
    for m, (real, imag) in enumerate(far):
        far_high[s, m], far_low[s, m] = hilo(columns([real * factor, imag * factor]))


def backward(s, probe, table_right, table_left, patch, psi, far_high, far_low, sums):
    num_re, num_im = jnp.zeros((W, W), F32), jnp.zeros((W, W), F32)
    for g in range(0, probe.shape[0], 2):
        high, low = rows_of([far_high[s, g], far_high[s, g + 1]]), rows_of([far_low[s, g], far_low[s, g + 1]])
        pairs = times_left(times_right(high, low, table_right), table_left)
        for m, (real, imag) in zip((g, g + 1), pairs):
            chi_re, chi_im = real - psi[s, m, 0], imag - psi[s, m, 1]
            num_re = num_re + (probe[m, 0] * chi_re + probe[m, 1] * chi_im)
            num_im = num_im + (probe[m, 0] * chi_im - probe[m, 1] * chi_re)
            add_plane(sums, 2 * m, patch[s, 0] * chi_re + patch[s, 1] * chi_im)
            add_plane(sums, 2 * m + 1, patch[s, 0] * chi_im - patch[s, 1] * chi_re)
    return num_re, num_im


DEPTH = 8
PLANE_STEPS = sorted(
    ((dx, dy) for dx in range(4) for dy in range(4) if dx + dy > 0),
    key=lambda step: -(min(step[0], 4 - step[0]) + min(step[1], 4 - step[1])),
)
DEPTH_STEPS = sorted(range(1, DEPTH), key=lambda step: -min(step, DEPTH - step))
UNIT = W // 8
TILES = 10 * UNIT
HALF = TILES // 2
SHARE = HALF // PLANE


def add_plane(sums, plane, value):
    here = pl.ds(plane * UNIT, UNIT)
    sums[here] += value.reshape(UNIT, 8, W)


def placed(shifted, plane, place, count, acc, target):
    lane = lax.broadcasted_iota(jnp.int32, (W, W), 1)
    for part in range(3):

        def add(s, blocks):
            top, left, live = place(s)
            value = shifted[s, plane, pl.ds(2 * W + part * W - top, W), :]
            out = []
            for j, block in enumerate(blocks):
                at = lane + (j * W - left)
                inside = jnp.logical_and(at >= 0, at < live * W)
                out.append(block + jnp.where(inside, value, 0.0))
            return tuple(out)

        blocks = lax.fori_loop(0, count, add, tuple(jnp.zeros((W, W), F32) for _ in range(3)), unroll=True)
        for j in range(3):
            acc[target, j, pl.ds(part * W, W), :] = blocks[j]


def step_kernel(rows, cols, offsets_hbm, counts_hbm, *refs):
    (obj, *hbm), (updated, direction) = refs[:7], refs[7:9]
    (offsets, counts, patch, psi, far_high, far_low, shifted, acc, sums, got, gathered, shard, layers, total) = refs[9:23]
    (from_left, from_above, from_corner, from_high, relay, halo_relay) = refs[23:29]
    (load, halo_send, halo_recv, send, recv, ar_send, ar_recv, ext, *vmem) = refs[29:]
    probe, amps, right_fwd, right_inv, left_fwd, left_inv = vmem
    slot_count = amps.shape[0]
    r, c = position()
    core, z_lo = lax.rem(r, 2), r // 2
    z_hi, xy = c // PLANE, lax.rem(c, PLANE)
    z = z_hi * (DEPTH // 2) + z_lo
    left, up = c > 0, r > 0
    right, down = c < cols - 1, r < rows - 1
    up_left, down_right = jnp.logical_and(up, left), jnp.logical_and(down, right)
    near_right, near_left = jnp.logical_and(right, c != PLANE - 1), jnp.logical_and(left, c != PLANE)
    up_right, turning = jnp.logical_and(up, near_right), jnp.logical_and(down, near_right)
    source, target = c == PLANE - 1, c == PLANE
    target_up = jnp.logical_and(target, up)
    passing = [c == spot for spot in SUMS_RELAYS]
    passing = passing[:2] + [jnp.logical_and(flag, down) for flag in passing[2:]]
    sourced = [source] * 2 + [jnp.logical_and(source, down)] * 2
    east, south, southeast = (r, c + 1), (r + 1, c), (r + 1, c + 1)
    twin = (r + 1 - 2 * core, c)

    def in_plane(k):
        dx, dy = PLANE_STEPS[k - 1]
        other = lax.rem(xy // 4 + dx, 4) * 4 + lax.rem(xy + dy, 4)
        return other, (r, z_hi * PLANE + other)

    def in_depth(k):
        other = lax.rem(z + DEPTH_STEPS[k - 1], DEPTH)
        half = DEPTH // 2
        return lax.rem(other, half) * 2 + core, (other // half) * PLANE + xy

    pieces = [(obj.at[:, :, pl.ds(k * W, W)], ext.at[:, k, pl.ds(0, 2 * W)]) for k in range(2)]
    pieces += [(offsets_hbm, offsets), (counts_hbm, counts)]
    pieces += list(zip(hbm, vmem))
    copies = [pltpu.make_async_copy(src, dst, load.at[k]) for k, (src, dst) in enumerate(pieces)]
    for copy in copies:
        copy.start()

    barrier = pltpu.get_barrier_semaphore()
    peers = [twin] + [in_plane(k)[1] for k in range(1, PLANE)] + [in_depth(k) for k in range(1, DEPTH)]
    ahead = [c == PLANE + spot for spot in HALO_RELAYS]
    ahead_up = [jnp.logical_and(flag, up) for flag in ahead]
    target_down = jnp.logical_and(source, down)
    greetings = [(source, (r, PLANE + spot)) for spot in HALO_RELAYS]
    greetings += [(target_down, (r + 1, PLANE + spot)) for spot in HALO_RELAYS]
    greetings += [(flag, (r, PLANE)) for flag in ahead] + [(near_right, east), (down, south)]
    waits = [near_left, up, *[target for _ in HALO_RELAYS], *ahead, *ahead_up]
    greetings += [(left, (r, c - 1)), (up, (r - 1, c)), (up_left, (r - 1, c - 1))]
    greetings += [(target, (r, spot)) for spot in SUMS_RELAYS[:2]]
    greetings += [(target_up, (r - 1, spot)) for spot in SUMS_RELAYS[2:]]
    greetings += [(flag, (r, PLANE - 1)) for flag in passing]
    for when, device in greetings:

        @pl.when(when)
        def _():
            pl.semaphore_signal(barrier, inc=1, device_id=device, device_id_type=MESH)

    for device in peers:
        pl.semaphore_signal(barrier, inc=1, device_id=device, device_id_type=MESH)
    waits += [right, down, down_right, *sourced, *passing]

    def place(s):
        return offsets[0, s], offsets[1, s], (s < counts[0, 0]).astype(jnp.int32)

    def remote(k, j, src, dst, device):
        return pltpu.make_async_remote_copy(src, dst, send.at[k], recv.at[j], device_id=device, device_id_type=MESH)

    def landed(when, ref, semaphore):
        wait = pltpu.make_async_copy(ref, ref, semaphore).wait
        if when is None:
            wait()
        else:
            pl.when(when)(wait)

    def summed(k, src, dst, device):
        return pltpu.make_async_remote_copy(src, dst, ar_send.at[k], ar_recv.at[k], device_id=device, device_id_type=MESH)

    def halo(k, j, src, dst, device):
        return pltpu.make_async_remote_copy(
            src, dst, halo_send.at[k], halo_recv.at[j], device_id=device, device_id_type=MESH
        )

    upper, lower, under_rows = pl.ds(0, W), pl.ds(W, W), pl.ds(2 * W, W)
    west, north = (r, c - 1), (r - 1, c)
    exchange = [
        (near_left, near_right, halo(0, 0, ext.at[:, 0, upper], ext.at[:, 2, upper], west)),
        (up, down, halo(1, 1, ext.at[:, 0, upper], ext.at[:, 0, under_rows], north)),
        (up, down, halo(2, 2, ext.at[:, 1, upper], ext.at[:, 1, under_rows], north)),
        (near_left, near_right, halo(3, 3, ext.at[:, 0, lower], ext.at[:, 2, lower], west)),
    ]
    handed = halo(4, 4, ext.at[:, 2, upper], ext.at[:, 2, under_rows], north)
    relays = len(HALO_RELAYS)
    share = 2 * W // relays
    there, back, above = [], [], []
    for half in range(2):
        for i, spot in enumerate(HALO_RELAYS):
            plane, start = i % 2, i // 2 * share
            span = pl.ds(half * W + start, share)
            held = halo_relay.at[half]
            there.append((target, ahead[i], halo(5, 5 + half, ext.at[plane, 0, span], held, (r, PLANE + spot))))
            back.append((ahead[i], source, halo(6 + half, 7 + half, held, ext.at[plane, 2, span], (r, PLANE - 1))))
            if half == 0:
                corner_rows = ext.at[plane, 2, pl.ds(2 * W + start, share)]
                above.append((ahead_up[i], target_down, halo(8, 9, held, corner_rows, (r - 1, PLANE - 1))))
    for copy in copies[:2]:
        copy.wait()
    pl.semaphore_wait(barrier, len(peers) + count(*waits))
    for sends, _, copy in there + exchange:
        pl.when(sends)(copy.start)

    shifted[...] = jnp.zeros_like(shifted)
    sums[...] = jnp.zeros_like(sums)
    for copy in copies[2:]:
        copy.wait()

    power = jnp.zeros((W, W), F32)
    for m in range(probe.shape[0]):
        power = power + (probe[m, 0] * probe[m, 0] + probe[m, 1] * probe[m, 1])

    def weigh(s, carry):
        shifted[s, 2, pl.ds(2 * W, W), :] = pltpu.roll(power, place(s)[1] % W, 1)
        return carry

    lax.fori_loop(0, slot_count, weigh, 0, unroll=True)
    placed(shifted, 2, place, slot_count, acc, 2)
    strip, under, corner = acc.at[:, 2, pl.ds(0, 2 * W)], acc.at[:, pl.ds(0, 2), pl.ds(2 * W, W)], acc.at[:, 2, pl.ds(2 * W, W)]
    weights = [
        (right, left, remote(0, 0, strip.at[2], from_left.at[2], east)),
        (down, up, remote(1, 1, under.at[2], from_above.at[2], south)),
        (down_right, up_left, remote(2, 2, corner.at[2], from_corner.at[2], southeast)),
    ]
    for sends, _, copy in weights:
        pl.when(sends)(copy.start)

    for (_, flag, arriving), (_, _, leaving) in zip(there, back):

        @pl.when(flag)
        def _():
            arriving.wait_recv()
            leaving.start()

    for flag, _, copy in above:
        pl.when(flag)(copy.start)
    pl.when(near_right)(exchange[0][2].wait_recv)
    pl.when(up_right)(handed.start)
    for _, receives, copy in exchange[1:] + [(up_right, turning, handed)]:
        pl.when(receives)(copy.wait_recv)
    landed(source, ext.at[:, 2, upper], halo_recv.at[7])
    landed(source, ext.at[:, 2, lower], halo_recv.at[8])
    landed(target_down, ext.at[:, 2, under_rows], halo_recv.at[9])

    def first(s, carry):
        forward(s, place(s), ext, probe, amps, right_fwd, left_fwd, patch, psi, far_high, far_low, sums)
        return carry

    lax.fori_loop(0, slot_count, first, 0, unroll=True)

    def second(s, carry):
        turn = place(s)[1] % W
        for plane, value in enumerate(backward(s, probe, right_inv, left_inv, patch, psi, far_high, far_low, sums)):
            shifted[s, plane, pl.ds(2 * W, W), :] = pltpu.roll(value, turn, 1)
        return carry

    lax.fori_loop(0, slot_count, second, 0, unroll=True)

    mine = pl.ds(core * HALF, HALF)
    swap = summed(0, sums.at[pl.ds((1 - core) * HALF, HALF)], got, twin)
    swap.start()
    placed(shifted, 0, place, slot_count, acc, 0)
    swap.wait_recv()
    got[...] += sums[mine]

    for k in range(1, PLANE):
        other, device = in_plane(k)
        summed(1, got.at[pl.ds(other * SHARE, SHARE)], gathered.at[k - 1], device).start()
    placed(shifted, 1, place, slot_count, acc, 1)
    numer = pl.ds(0, 2)
    crossing = [(strip.at[p, lower], from_left.at[p, lower], (r, PLANE)) for p in range(2)]
    crossing += [(corner.at[p], from_corner.at[p], (r + 1, PLANE)) for p in range(2)]
    pass_on = [remote(3 + i, 3, src, relay, (r, spot)) for i, ((src, _, _), spot) in enumerate(zip(crossing, SUMS_RELAYS))]
    passed = [remote(7, 4 + i // 2, relay, dst, device) for i, (_, dst, device) in enumerate(crossing)]
    turned = remote(8, 6, corner.at[numer], from_high, south)
    plan = [
        (turning, up_right, turned),
        (near_right, near_left, remote(9, 7, strip.at[numer, lower], from_left.at[numer, lower], east)),
        (down, up, remote(10, 8, under.at[numer], from_above.at[numer], south)),
    ]
    late = remote(11, 9, strip.at[numer, upper], from_left.at[numer, upper], east)
    for flag, copy in zip(sourced, pass_on):
        pl.when(flag)(copy.start)
    pl.when(source)(late.start)
    for sends, _, copy in plan:
        pl.when(sends)(copy.start)
    value = got[pl.ds(xy * SHARE, SHARE)]
    landed(None, gathered, ar_recv.at[1])
    for k in range(1, PLANE):
        value = value + gathered[k - 1]
    shard[...] = value

    for k in range(1, DEPTH):
        summed(2, shard, layers.at[z], in_depth(k)).start()
    layers[z] = value
    for flag, arriving, leaving in zip(passing, pass_on, passed):

        @pl.when(flag)
        def _():
            arriving.wait_recv()
            leaving.start()

    @pl.when(up_right)
    def _():
        turned.wait_recv()
        strip[numer, upper] += from_high[...]

    pl.when(near_right)(late.start)
    landed(None, layers.at[pl.ds(0, DEPTH - 1)], ar_recv.at[2])
    value = layers[0]
    for k in range(1, DEPTH):
        value = value + layers[k]
    here = pl.ds(core * HALF + xy * SHARE, SHARE)
    total[here] = value

    for k in range(1, PLANE):
        summed(3, total.at[here], total.at[here], in_plane(k)[1]).start()

    others = pl.ds(core * HALF, HALF - SHARE)
    landed(None, total.at[others], ar_recv.at[3])
    half = total.at[mine]
    last = summed(4, half, half, twin)
    last.start()

    for _, receives, copy in weights + plan[1:]:
        pl.when(receives)(copy.wait_recv)
    landed(target, from_left.at[numer, lower], recv.at[4])
    landed(target_up, from_corner.at[numer], recv.at[5])
    pl.when(left)(late.wait_recv)

    def taken(flag, value):
        return jnp.where(jnp.broadcast_to(flag.astype(jnp.int32), value.shape) > 0, value, 0.0)

    for i in range(2):
        for j in range(2):
            span = pl.ds(i * W, W)
            parts = []
            for plane in range(3):
                value = acc[plane, j, span, :]
                if j == 0:
                    value = value + taken(left, from_left[plane, span, :])
                if i == 0:
                    value = value + taken(up, from_above[plane, j])
                if i == 0 and j == 0:
                    value = value + taken(up_left if plane == 2 else target_up, from_corner[plane])
                parts.append(value)
            scale = 1.0 / (parts[2] + 1.0)
            for plane in range(2):
                updated[plane, span, pl.ds(j * W, W)] = ext[plane, j, span, :] + parts[plane] * scale

    last.wait_recv()
    scale = lax.rsqrt(total[pl.ds(8 * UNIT, UNIT)] + 1.0)
    for plane in range(8):
        direction[plane] = total[pl.ds(plane * UNIT, UNIT)] * scale
    for copy in [swap, last]:
        copy.wait_send()
    landed(None, got.at[pl.ds(0, HALF - SHARE)], ar_send.at[1])
    landed(None, layers.at[pl.ds(0, DEPTH - 1)], ar_send.at[2])
    landed(None, total.at[others], ar_send.at[3])
    for sends, _, copy in exchange + back + above + [(up_right, turning, handed)] + weights + plan:
        pl.when(sends)(copy.wait_send)
    landed(target, ext.at[:, 0, pl.ds(0, 2 * W)], halo_send.at[5])
    for flag, copy in zip(sourced + passing, pass_on + passed):
        pl.when(flag)(copy.wait_send)
    pl.when(right)(late.wait_send)


def step(obj, probe, offsets, counts, amps, rows, cols):
    fwd, inv = tables()
    consts = [
        np.concatenate([fwd[0], fwd[0], fwd[1]], 0),
        np.concatenate([inv[0], inv[0], inv[1]], 0),
        np.concatenate([inv[0], inv[1]], 0),
        np.concatenate([fwd[0], fwd[1]], 0),
    ]
    loaded = [probe, amps] + [jnp.asarray(v) for v in consts]
    slot_count, modes = amps.shape[0], probe.shape[0]
    dma = pltpu.SemaphoreType.DMA
    messages = 5
    return pl.pallas_call(
        functools.partial(step_kernel, rows, cols),
        out_shape=(
            pltpu.VMEM(obj.shape, F32),
            pltpu.VMEM((8, UNIT, 8, W), F32),
        ),
        in_specs=[HBM] * 9,
        out_specs=(VMEM, VMEM),
        scratch_shapes=[
            pltpu.SMEM(offsets.shape[::-1], jnp.int32),
            pltpu.SMEM((1, 1), jnp.int32),
            pltpu.VMEM((slot_count, 2, W, W), F32),
            pltpu.VMEM((slot_count, modes, 2, W, W), F32),
            pltpu.VMEM((slot_count, modes, W, 2 * W), BF),
            pltpu.VMEM((slot_count, modes, W, 2 * W), BF),
            pltpu.VMEM((slot_count, 3, 5 * W, W), F32),
            pltpu.VMEM((3, 3, 3 * W, W), F32),
            pltpu.VMEM((TILES, 8, W), F32),
            pltpu.VMEM((HALF, 8, W), F32),
            pltpu.VMEM((PLANE - 1, SHARE, 8, W), F32),
            pltpu.VMEM((SHARE, 8, W), F32),
            pltpu.VMEM((DEPTH, SHARE, 8, W), F32),
            pltpu.VMEM((TILES, 8, W), F32),
            pltpu.VMEM((3, 2 * W, W), F32),
            pltpu.VMEM((3, 2, W, W), F32),
            pltpu.VMEM((3, W, W), F32),
            pltpu.VMEM((2, W, W), F32),
            pltpu.VMEM((W, W), F32),
            pltpu.VMEM((2, 2 * W // len(HALO_RELAYS), W), F32),
            dma((10,)),
            dma((9,)),
            dma((10,)),
            dma((12,)),
            dma((10,)),
            dma((messages,)),
            dma((messages,)),
            pltpu.VMEM((2, 3, 3 * W, W), F32),
        ]
        + [pltpu.VMEM(v.shape, v.dtype) for v in loaded],
        compiler_params=pltpu.CompilerParams(collective_id=0, has_side_effects=True, vmem_limit_bytes=LIMIT),
        name="step",
    )(offsets.T, counts[None], obj, *loaded)


def finish_kernel(held_object, held_direction, new_object, direction, done):
    copies = [
        pltpu.make_async_copy(held_object, new_object, done.at[0]),
        pltpu.make_async_copy(held_direction, direction, done.at[1]),
    ]
    for copy in copies:
        copy.start()
    for copy in copies:
        copy.wait()


def finish(held_object, held_direction):
    return pl.pallas_call(
        finish_kernel,
        out_shape=(
            jax.ShapeDtypeStruct(held_object.shape, F32),
            jax.ShapeDtypeStruct(held_direction.shape, F32),
        ),
        in_specs=[VMEM, VMEM],
        out_specs=(HBM, HBM),
        scratch_shapes=[pltpu.SemaphoreType.DMA((2,))],
        compiler_params=pltpu.CompilerParams(vmem_limit_bytes=16 * 2**20),
        name="finish",
    )(held_object, held_direction)


def body(rows, cols, object_field, probe, offsets, counts, amplitudes):
    held = step(object_field, probe, offsets, counts, amplitudes, rows, cols)
    new_object, direction = finish(*held)
    return new_object, direction.reshape(probe.shape)


def solution(mesh):
    rows, cols = mesh.shape["row"], mesh.shape["col"]
    return jax.shard_map(
        functools.partial(body, rows, cols),
        mesh=mesh,
        in_specs=(
            P(None, "row", "col"),
            P(),
            P(("row", "col"), None),
            P(("row", "col")),
            P(("row", "col"), None, None),
        ),
        out_specs=(P(None, "row", "col"), P()),
        check_vma=False,
    )
```

```python
import functools

import jax
import jax.numpy as jnp
import ml_dtypes
import numpy as np
from jax import lax
from jax.experimental import pallas as pl
from jax.experimental.pallas import tpu as pltpu
from jax.sharding import PartitionSpec as P

BF = jnp.bfloat16
F32 = jnp.float32
W = 128
MESH = pl.DeviceIdType.MESH
HBM = pl.BlockSpec(memory_space=pl.ANY)
VMEM = pl.BlockSpec(memory_space=pltpu.VMEM)
SMEM = pl.BlockSpec(memory_space=pltpu.SMEM)
LIMIT = 56 * 2**20


def tables():
    index = np.arange(W)
    angle = (index[:, None] * index[None, :] % W) * (2 * np.pi / W)
    cosine, sine = np.cos(angle) / np.sqrt(W), np.sin(angle) / np.sqrt(W)

    def split(matrix):
        matrix = matrix.astype(np.float32)
        high = matrix.astype(ml_dtypes.bfloat16)
        return high, (matrix - high.astype(np.float32)).astype(ml_dtypes.bfloat16)

    fwd = split(np.block([[cosine, -sine], [sine, cosine]]))
    inv = split(np.block([[cosine, sine], [-sine, cosine]]))
    return fwd, inv


def position():
    return lax.axis_index("row"), lax.axis_index("col")


def count(*flags):
    return sum(flag.astype(jnp.int32) for flag in flags)


PLANE = 16
HALO_RELAYS = (12, 4, 1, 3, 15, 5, 13, 7)
SUMS_RELAYS = (0, 12, 13, 14)


def hilo(x):
    high = x.astype(BF)
    return high, (x - high.astype(F32)).astype(BF)


def dot(a, b):
    return jnp.dot(a, b, preferred_element_type=F32)


def columns(parts):
    return jnp.concatenate(parts, axis=1)


def rows_of(parts):
    return jnp.concatenate(parts, axis=0)


def times_right(high, low, table):
    out = dot(columns([high, low, high]), table[...])
    return [(out[k * W : (k + 1) * W, :W], out[k * W : (k + 1) * W, W:]) for k in range(2)]


def times_left(pairs, table):
    high, low = hilo(columns([rows_of(pair) for pair in pairs]))
    out = dot(table[...], high)
    out = out[: 2 * W] + out[2 * W :] + dot(table[: 2 * W], low)
    return [(out[:W, k * W : (k + 1) * W], out[W:, k * W : (k + 1) * W]) for k in range(2)]


def forward(s, place, ext, probe, amps, table_right, table_left, patch, psi, far_high, far_low, sums):
    top, left, live = place
    block, lanes = left // W, left % W
    lane = lax.broadcasted_iota(jnp.int32, (W, W), 1)
    kept = lane < live * W

    def cut(plane):
        first = ext[plane, block, pl.ds(top, W), :]
        second = ext[plane, block + 1, pl.ds(top, W), :]
        turned = pltpu.roll(jnp.where(lane >= lanes, first, second), (W - lanes) % W, 1)
        return jnp.where(kept, turned, 0.0)

    ore, oim = cut(0), cut(1)
    patch[s, 0], patch[s, 1] = ore, oim
    add_plane(sums, 8, ore * ore + oim * oim)
    inten = jnp.zeros((W, W), F32)
    far = []
    for g in range(0, probe.shape[0], 2):
        for m in (g, g + 1):
            psi[s, m, 0] = probe[m, 0] * ore - probe[m, 1] * oim
            psi[s, m, 1] = probe[m, 0] * oim + probe[m, 1] * ore
        high, low = hilo(rows_of([columns([psi[s, m, 0], psi[s, m, 1]]) for m in (g, g + 1)]))
        pairs = times_left(times_right(high, low, table_right), table_left)
        for real, imag in pairs:
            inten = inten + (real * real + imag * imag)
        far += pairs
    factor = amps[s] * lax.rsqrt(jnp.maximum(inten, 0.25))
    for m, (real, imag) in enumerate(far):
        far_high[s, m], far_low[s, m] = hilo(columns([real * factor, imag * factor]))


def backward(s, probe, table_right, table_left, patch, psi, far_high, far_low, sums):
    num_re, num_im = jnp.zeros((W, W), F32), jnp.zeros((W, W), F32)
    for g in range(0, probe.shape[0], 2):
        high, low = rows_of([far_high[s, g], far_high[s, g + 1]]), rows_of([far_low[s, g], far_low[s, g + 1]])
        pairs = times_left(times_right(high, low, table_right), table_left)
        for m, (real, imag) in zip((g, g + 1), pairs):
            chi_re, chi_im = real - psi[s, m, 0], imag - psi[s, m, 1]
            num_re = num_re + (probe[m, 0] * chi_re + probe[m, 1] * chi_im)
            num_im = num_im + (probe[m, 0] * chi_im - probe[m, 1] * chi_re)
            add_plane(sums, 2 * m, patch[s, 0] * chi_re + patch[s, 1] * chi_im)
            add_plane(sums, 2 * m + 1, patch[s, 0] * chi_im - patch[s, 1] * chi_re)
    return num_re, num_im


DEPTH = 8
PLANE_STEPS = sorted(
    ((dx, dy) for dx in range(4) for dy in range(4) if dx + dy > 0),
    key=lambda step: -(min(step[0], 4 - step[0]) + min(step[1], 4 - step[1])),
)
DEPTH_STEPS = sorted(range(1, DEPTH), key=lambda step: -min(step, DEPTH - step))
UNIT = W // 8
TILES = 10 * UNIT
HALF = TILES // 2
SHARE = HALF // PLANE


def add_plane(sums, plane, value):
    here = pl.ds(plane * UNIT, UNIT)
    sums[here] += value.reshape(UNIT, 8, W)


def placed(shifted, plane, place, count, acc, target):
    lane = lax.broadcasted_iota(jnp.int32, (W, W), 1)
    for part in range(3):

        def add(s, blocks):
            top, left, live = place(s)
            value = shifted[s, plane, pl.ds(2 * W + part * W - top, W), :]
            out = []
            for j, block in enumerate(blocks):
                at = lane + (j * W - left)
                inside = jnp.logical_and(at >= 0, at < live * W)
                out.append(block + jnp.where(inside, value, 0.0))
            return tuple(out)

        blocks = lax.fori_loop(0, count, add, tuple(jnp.zeros((W, W), F32) for _ in range(3)), unroll=True)
        for j in range(3):
            acc[target, j, pl.ds(part * W, W), :] = blocks[j]


def step_kernel(rows, cols, offsets_hbm, counts_hbm, *refs):
    (obj, *hbm), (updated, direction) = refs[:7], refs[7:9]
    (offsets, counts, patch, psi, far_high, far_low, shifted, acc, sums, got, gathered, shard, layers, total) = refs[9:23]
    (from_left, from_above, from_corner, from_high, relay, halo_relay) = refs[23:29]
    (load, halo_send, halo_recv, send, recv, ar_send, ar_recv, ext, *vmem) = refs[29:]
    probe, amps, right_fwd, right_inv, left_fwd, left_inv = vmem
    slot_count = amps.shape[0]
    r, c = position()
    core, z_lo = lax.rem(r, 2), r // 2
    z_hi, xy = c // PLANE, lax.rem(c, PLANE)
    z = z_hi * (DEPTH // 2) + z_lo
    left, up = c > 0, r > 0
    right, down = c < cols - 1, r < rows - 1
    up_left, down_right = jnp.logical_and(up, left), jnp.logical_and(down, right)
    near_right, near_left = jnp.logical_and(right, c != PLANE - 1), jnp.logical_and(left, c != PLANE)
    up_right, turning = jnp.logical_and(up, near_right), jnp.logical_and(down, near_right)
    source, target = c == PLANE - 1, c == PLANE
    target_up = jnp.logical_and(target, up)
    passing = [c == spot for spot in SUMS_RELAYS]
    passing = passing[:2] + [jnp.logical_and(flag, down) for flag in passing[2:]]
    sourced = [source] * 2 + [jnp.logical_and(source, down)] * 2
    east, south, southeast = (r, c + 1), (r + 1, c), (r + 1, c + 1)
    twin = (r + 1 - 2 * core, c)

    def in_plane(k):
        dx, dy = PLANE_STEPS[k - 1]
        other = lax.rem(xy // 4 + dx, 4) * 4 + lax.rem(xy + dy, 4)
        return other, (r, z_hi * PLANE + other)

    def in_depth(k):
        other = lax.rem(z + DEPTH_STEPS[k - 1], DEPTH)
        half = DEPTH // 2
        return lax.rem(other, half) * 2 + core, (other // half) * PLANE + xy

    pieces = [(obj.at[:, :, pl.ds(k * W, W)], ext.at[:, k, pl.ds(0, 2 * W)]) for k in range(2)]
    pieces += [(offsets_hbm, offsets), (counts_hbm, counts)]
    pieces += list(zip(hbm, vmem))
    copies = [pltpu.make_async_copy(src, dst, load.at[k]) for k, (src, dst) in enumerate(pieces)]
    for copy in copies:
        copy.start()

    barrier = pltpu.get_barrier_semaphore()
    peers = [twin] + [in_plane(k)[1] for k in range(1, PLANE)] + [in_depth(k) for k in range(1, DEPTH)]
    ahead = [c == PLANE + spot for spot in HALO_RELAYS]
    ahead_up = [jnp.logical_and(flag, up) for flag in ahead]
    target_down = jnp.logical_and(source, down)
    greetings = [(source, (r, PLANE + spot)) for spot in HALO_RELAYS]
    greetings += [(target_down, (r + 1, PLANE + spot)) for spot in HALO_RELAYS]
    greetings += [(flag, (r, PLANE)) for flag in ahead] + [(near_right, east), (down, south)]
    waits = [near_left, up, *[target for _ in HALO_RELAYS], *ahead, *ahead_up]
    greetings += [(left, (r, c - 1)), (up, (r - 1, c)), (up_left, (r - 1, c - 1))]
    greetings += [(target, (r, spot)) for spot in SUMS_RELAYS[:2]]
    greetings += [(target_up, (r - 1, spot)) for spot in SUMS_RELAYS[2:]]
    greetings += [(flag, (r, PLANE - 1)) for flag in passing]
    for when, device in greetings:

        @pl.when(when)
        def _():
            pl.semaphore_signal(barrier, inc=1, device_id=device, device_id_type=MESH)

    for device in peers:
        pl.semaphore_signal(barrier, inc=1, device_id=device, device_id_type=MESH)
    waits += [right, down, down_right, *sourced, *passing]

    def place(s):
        return offsets[0, s], offsets[1, s], (s < counts[0, 0]).astype(jnp.int32)

    def remote(k, j, src, dst, device):
        return pltpu.make_async_remote_copy(src, dst, send.at[k], recv.at[j], device_id=device, device_id_type=MESH)

    def landed(when, ref, semaphore):
        wait = pltpu.make_async_copy(ref, ref, semaphore).wait
        if when is None:
            wait()
        else:
            pl.when(when)(wait)

    def summed(k, src, dst, device):
        return pltpu.make_async_remote_copy(src, dst, ar_send.at[k], ar_recv.at[k], device_id=device, device_id_type=MESH)

    def halo(k, j, src, dst, device):
        return pltpu.make_async_remote_copy(
            src, dst, halo_send.at[k], halo_recv.at[j], device_id=device, device_id_type=MESH
        )

    upper, lower, under_rows = pl.ds(0, W), pl.ds(W, W), pl.ds(2 * W, W)
    west, north = (r, c - 1), (r - 1, c)
    exchange = [
        (near_left, near_right, halo(0, 0, ext.at[:, 0, upper], ext.at[:, 2, upper], west)),
        (up, down, halo(1, 1, ext.at[:, 0, upper], ext.at[:, 0, under_rows], north)),
        (up, down, halo(2, 2, ext.at[:, 1, upper], ext.at[:, 1, under_rows], north)),
        (near_left, near_right, halo(3, 3, ext.at[:, 0, lower], ext.at[:, 2, lower], west)),
    ]
    handed = halo(4, 4, ext.at[:, 2, upper], ext.at[:, 2, under_rows], north)
    relays = len(HALO_RELAYS)
    share = 2 * W // relays
    there, back, above = [], [], []
    for half in range(2):
        for i, spot in enumerate(HALO_RELAYS):
            plane, start = i % 2, i // 2 * share
            span = pl.ds(half * W + start, share)
            held = halo_relay.at[half]
            there.append((target, ahead[i], halo(5, 5 + half, ext.at[plane, 0, span], held, (r, PLANE + spot))))
            back.append((ahead[i], source, halo(6 + half, 7 + half, held, ext.at[plane, 2, span], (r, PLANE - 1))))
            if half == 0:
                corner_rows = ext.at[plane, 2, pl.ds(2 * W + start, share)]
                above.append((ahead_up[i], target_down, halo(8, 9, held, corner_rows, (r - 1, PLANE - 1))))
    for copy in copies[:2]:
        copy.wait()
    pl.semaphore_wait(barrier, len(peers) + count(*waits))
    for sends, _, copy in there + exchange:
        pl.when(sends)(copy.start)

    shifted[...] = jnp.zeros_like(shifted)
    sums[...] = jnp.zeros_like(sums)
    for copy in copies[2:]:
        copy.wait()

    power = jnp.zeros((W, W), F32)
    for m in range(probe.shape[0]):
        power = power + (probe[m, 0] * probe[m, 0] + probe[m, 1] * probe[m, 1])

    def weigh(s, carry):
        shifted[s, 2, pl.ds(2 * W, W), :] = pltpu.roll(power, place(s)[1] % W, 1)
        return carry

    lax.fori_loop(0, slot_count, weigh, 0, unroll=True)
    placed(shifted, 2, place, slot_count, acc, 2)
    strip, under, corner = acc.at[:, 2, pl.ds(0, 2 * W)], acc.at[:, pl.ds(0, 2), pl.ds(2 * W, W)], acc.at[:, 2, pl.ds(2 * W, W)]
    weights = [
        (right, left, remote(0, 0, strip.at[2], from_left.at[2], east)),
        (down, up, remote(1, 1, under.at[2], from_above.at[2], south)),
        (down_right, up_left, remote(2, 2, corner.at[2], from_corner.at[2], southeast)),
    ]
    for (_, flag, arriving), (_, _, leaving) in zip(there, back):

        @pl.when(flag)
        def _():
            arriving.wait_recv()
            leaving.start()

    for flag, _, copy in above:
        pl.when(flag)(copy.start)
    pl.when(near_right)(exchange[0][2].wait_recv)
    pl.when(up_right)(handed.start)
    for _, receives, copy in exchange[1:] + [(up_right, turning, handed)]:
        pl.when(receives)(copy.wait_recv)
    landed(source, ext.at[:, 2, upper], halo_recv.at[7])
    landed(source, ext.at[:, 2, lower], halo_recv.at[8])
    landed(target_down, ext.at[:, 2, under_rows], halo_recv.at[9])
    for sends, _, copy in weights:
        pl.when(sends)(copy.start)

    def first(s, carry):
        forward(s, place(s), ext, probe, amps, right_fwd, left_fwd, patch, psi, far_high, far_low, sums)
        return carry

    lax.fori_loop(0, slot_count, first, 0, unroll=True)

    def second(s, carry):
        turn = place(s)[1] % W
        for plane, value in enumerate(backward(s, probe, right_inv, left_inv, patch, psi, far_high, far_low, sums)):
            shifted[s, plane, pl.ds(2 * W, W), :] = pltpu.roll(value, turn, 1)
        return carry

    lax.fori_loop(0, slot_count, second, 0, unroll=True)

    mine = pl.ds(core * HALF, HALF)
    swap = summed(0, sums.at[pl.ds((1 - core) * HALF, HALF)], got, twin)
    swap.start()
    placed(shifted, 0, place, slot_count, acc, 0)
    swap.wait_recv()
    got[...] += sums[mine]

    for k in range(1, PLANE):
        other, device = in_plane(k)
        summed(1, got.at[pl.ds(other * SHARE, SHARE)], gathered.at[k - 1], device).start()
    placed(shifted, 1, place, slot_count, acc, 1)
    numer = pl.ds(0, 2)
    crossing = [(strip.at[p, lower], from_left.at[p, lower], (r, PLANE)) for p in range(2)]
    crossing += [(corner.at[p], from_corner.at[p], (r + 1, PLANE)) for p in range(2)]
    pass_on = [remote(3 + i, 3, src, relay, (r, spot)) for i, ((src, _, _), spot) in enumerate(zip(crossing, SUMS_RELAYS))]
    passed = [remote(7, 4 + i // 2, relay, dst, device) for i, (_, dst, device) in enumerate(crossing)]
    turned = remote(8, 6, corner.at[numer], from_high, south)
    plan = [
        (turning, up_right, turned),
        (near_right, near_left, remote(9, 7, strip.at[numer, lower], from_left.at[numer, lower], east)),
        (down, up, remote(10, 8, under.at[numer], from_above.at[numer], south)),
    ]
    late = remote(11, 9, strip.at[numer, upper], from_left.at[numer, upper], east)
    for flag, copy in zip(sourced, pass_on):
        pl.when(flag)(copy.start)
    pl.when(source)(late.start)
    for sends, _, copy in plan:
        pl.when(sends)(copy.start)
    value = got[pl.ds(xy * SHARE, SHARE)]
    landed(None, gathered, ar_recv.at[1])
    for k in range(1, PLANE):
        value = value + gathered[k - 1]
    shard[...] = value

    for k in range(1, DEPTH):
        summed(2, shard, layers.at[z], in_depth(k)).start()
    layers[z] = value
    for flag, arriving, leaving in zip(passing, pass_on, passed):

        @pl.when(flag)
        def _():
            arriving.wait_recv()
            leaving.start()

    @pl.when(up_right)
    def _():
        turned.wait_recv()
        strip[numer, upper] += from_high[...]

    pl.when(near_right)(late.start)
    landed(None, layers.at[pl.ds(0, DEPTH - 1)], ar_recv.at[2])
    value = layers[0]
    for k in range(1, DEPTH):
        value = value + layers[k]
    here = pl.ds(core * HALF + xy * SHARE, SHARE)
    total[here] = value

    for k in range(1, PLANE):
        summed(3, total.at[here], total.at[here], in_plane(k)[1]).start()

    others = pl.ds(core * HALF, HALF - SHARE)
    landed(None, total.at[others], ar_recv.at[3])
    half = total.at[mine]
    last = summed(4, half, half, twin)
    last.start()

    for _, receives, copy in weights + plan[1:]:
        pl.when(receives)(copy.wait_recv)
    landed(target, from_left.at[numer, lower], recv.at[4])
    landed(target_up, from_corner.at[numer], recv.at[5])
    pl.when(left)(late.wait_recv)

    def taken(flag, value):
        return jnp.where(jnp.broadcast_to(flag.astype(jnp.int32), value.shape) > 0, value, 0.0)

    for i in range(2):
        for j in range(2):
            span = pl.ds(i * W, W)
            parts = []
            for plane in range(3):
                value = acc[plane, j, span, :]
                if j == 0:
                    value = value + taken(left, from_left[plane, span, :])
                if i == 0:
                    value = value + taken(up, from_above[plane, j])
                if i == 0 and j == 0:
                    value = value + taken(up_left if plane == 2 else target_up, from_corner[plane])
                parts.append(value)
            scale = 1.0 / (parts[2] + 1.0)
            for plane in range(2):
                updated[plane, span, pl.ds(j * W, W)] = ext[plane, j, span, :] + parts[plane] * scale

    last.wait_recv()
    scale = lax.rsqrt(total[pl.ds(8 * UNIT, UNIT)] + 1.0)
    for plane in range(8):
        direction[plane] = total[pl.ds(plane * UNIT, UNIT)] * scale
    for copy in [swap, last]:
        copy.wait_send()
    landed(None, got.at[pl.ds(0, HALF - SHARE)], ar_send.at[1])
    landed(None, layers.at[pl.ds(0, DEPTH - 1)], ar_send.at[2])
    landed(None, total.at[others], ar_send.at[3])
    for sends, _, copy in exchange + back + above + [(up_right, turning, handed)] + weights + plan:
        pl.when(sends)(copy.wait_send)
    landed(target, ext.at[:, 0, pl.ds(0, 2 * W)], halo_send.at[5])
    for flag, copy in zip(sourced + passing, pass_on + passed):
        pl.when(flag)(copy.wait_send)
    pl.when(right)(late.wait_send)


def step(obj, probe, offsets, counts, amps, rows, cols):
    fwd, inv = tables()
    consts = [
        np.concatenate([fwd[0], fwd[0], fwd[1]], 0),
        np.concatenate([inv[0], inv[0], inv[1]], 0),
        np.concatenate([inv[0], inv[1]], 0),
        np.concatenate([fwd[0], fwd[1]], 0),
    ]
    loaded = [probe, amps] + [jnp.asarray(v) for v in consts]
    slot_count, modes = amps.shape[0], probe.shape[0]
    dma = pltpu.SemaphoreType.DMA
    messages = 5
    return pl.pallas_call(
        functools.partial(step_kernel, rows, cols),
        out_shape=(
            pltpu.VMEM(obj.shape, F32),
            pltpu.VMEM((8, UNIT, 8, W), F32),
        ),
        in_specs=[HBM] * 9,
        out_specs=(VMEM, VMEM),
        scratch_shapes=[
            pltpu.SMEM(offsets.shape[::-1], jnp.int32),
            pltpu.SMEM((1, 1), jnp.int32),
            pltpu.VMEM((slot_count, 2, W, W), F32),
            pltpu.VMEM((slot_count, modes, 2, W, W), F32),
            pltpu.VMEM((slot_count, modes, W, 2 * W), BF),
            pltpu.VMEM((slot_count, modes, W, 2 * W), BF),
            pltpu.VMEM((slot_count, 3, 5 * W, W), F32),
            pltpu.VMEM((3, 3, 3 * W, W), F32),
            pltpu.VMEM((TILES, 8, W), F32),
            pltpu.VMEM((HALF, 8, W), F32),
            pltpu.VMEM((PLANE - 1, SHARE, 8, W), F32),
            pltpu.VMEM((SHARE, 8, W), F32),
            pltpu.VMEM((DEPTH, SHARE, 8, W), F32),
            pltpu.VMEM((TILES, 8, W), F32),
            pltpu.VMEM((3, 2 * W, W), F32),
            pltpu.VMEM((3, 2, W, W), F32),
            pltpu.VMEM((3, W, W), F32),
            pltpu.VMEM((2, W, W), F32),
            pltpu.VMEM((W, W), F32),
            pltpu.VMEM((2, 2 * W // len(HALO_RELAYS), W), F32),
            dma((10,)),
            dma((9,)),
            dma((10,)),
            dma((12,)),
            dma((10,)),
            dma((messages,)),
            dma((messages,)),
            pltpu.VMEM((2, 3, 3 * W, W), F32),
        ]
        + [pltpu.VMEM(v.shape, v.dtype) for v in loaded],
        compiler_params=pltpu.CompilerParams(collective_id=0, has_side_effects=True, vmem_limit_bytes=LIMIT),
        name="step",
    )(offsets.T, counts[None], obj, *loaded)


def finish_kernel(held_object, held_direction, new_object, direction, done):
    copies = [
        pltpu.make_async_copy(held_object, new_object, done.at[0]),
        pltpu.make_async_copy(held_direction, direction, done.at[1]),
    ]
    for copy in copies:
        copy.start()
    for copy in copies:
        copy.wait()


def finish(held_object, held_direction):
    return pl.pallas_call(
        finish_kernel,
        out_shape=(
            jax.ShapeDtypeStruct(held_object.shape, F32),
            jax.ShapeDtypeStruct(held_direction.shape, F32),
        ),
        in_specs=[VMEM, VMEM],
        out_specs=(HBM, HBM),
        scratch_shapes=[pltpu.SemaphoreType.DMA((2,))],
        compiler_params=pltpu.CompilerParams(vmem_limit_bytes=16 * 2**20),
        name="finish",
    )(held_object, held_direction)


def body(rows, cols, object_field, probe, offsets, counts, amplitudes):
    held = step(object_field, probe, offsets, counts, amplitudes, rows, cols)
    new_object, direction = finish(*held)
    return new_object, direction.reshape(probe.shape)


def solution(mesh):
    rows, cols = mesh.shape["row"], mesh.shape["col"]
    return jax.shard_map(
        functools.partial(body, rows, cols),
        mesh=mesh,
        in_specs=(
            P(None, "row", "col"),
            P(),
            P(("row", "col"), None),
            P(("row", "col")),
            P(("row", "col"), None, None),
        ),
        out_specs=(P(None, "row", "col"), P()),
        check_vma=False,
    )
```

```python
import functools

import jax
import jax.numpy as jnp
import ml_dtypes
import numpy as np
from jax import lax
from jax.experimental import pallas as pl
from jax.experimental.pallas import tpu as pltpu
from jax.sharding import PartitionSpec as P

BF = jnp.bfloat16
F32 = jnp.float32
W = 128
MESH = pl.DeviceIdType.MESH
HBM = pl.BlockSpec(memory_space=pl.ANY)
VMEM = pl.BlockSpec(memory_space=pltpu.VMEM)
SMEM = pl.BlockSpec(memory_space=pltpu.SMEM)
LIMIT = 56 * 2**20


def tables():
    index = np.arange(W)
    angle = (index[:, None] * index[None, :] % W) * (2 * np.pi / W)
    cosine, sine = np.cos(angle) / np.sqrt(W), np.sin(angle) / np.sqrt(W)

    def split(matrix):
        matrix = matrix.astype(np.float32)
        high = matrix.astype(ml_dtypes.bfloat16)
        return high, (matrix - high.astype(np.float32)).astype(ml_dtypes.bfloat16)

    fwd = split(np.block([[cosine, -sine], [sine, cosine]]))
    inv = split(np.block([[cosine, sine], [-sine, cosine]]))
    return fwd, inv


def position():
    return lax.axis_index("row"), lax.axis_index("col")


def count(*flags):
    return sum(flag.astype(jnp.int32) for flag in flags)


PLANE = 16
HALO_RELAYS = (12, 4, 1, 3, 15, 5, 13, 7)
SUMS_RELAYS = (0, 12, 13, 14)


def hilo(x):
    high = x.astype(BF)
    return high, (x - high.astype(F32)).astype(BF)


def dot(a, b):
    return jnp.dot(a, b, preferred_element_type=F32)


def columns(parts):
    return jnp.concatenate(parts, axis=1)


def rows_of(parts):
    return jnp.concatenate(parts, axis=0)


def times_right(high, low, table):
    out = dot(columns([high, low, high]), table[...])
    return [(out[k * W : (k + 1) * W, :W], out[k * W : (k + 1) * W, W:]) for k in range(2)]


def times_left(pairs, table):
    high, low = hilo(columns([rows_of(pair) for pair in pairs]))
    out = dot(table[...], high)
    out = out[: 2 * W] + out[2 * W :] + dot(table[: 2 * W], low)
    return [(out[:W, k * W : (k + 1) * W], out[W:, k * W : (k + 1) * W]) for k in range(2)]


def forward(s, place, ext, probe, amps, table_right, table_left, patch, psi, far_high, far_low, sums):
    top, left, live = place
    block, lanes = left // W, left % W
    lane = lax.broadcasted_iota(jnp.int32, (W, W), 1)
    kept = lane < live * W

    def cut(plane):
        first = ext[plane, block, pl.ds(top, W), :]
        second = ext[plane, block + 1, pl.ds(top, W), :]
        turned = pltpu.roll(jnp.where(lane >= lanes, first, second), (W - lanes) % W, 1)
        return jnp.where(kept, turned, 0.0)

    ore, oim = cut(0), cut(1)
    patch[s, 0], patch[s, 1] = ore, oim
    add_plane(sums, 8, ore * ore + oim * oim)
    inten = jnp.zeros((W, W), F32)
    far = []
    for g in range(0, probe.shape[0], 2):
        for m in (g, g + 1):
            psi[s, m, 0] = probe[m, 0] * ore - probe[m, 1] * oim
            psi[s, m, 1] = probe[m, 0] * oim + probe[m, 1] * ore
        high, low = hilo(rows_of([columns([psi[s, m, 0], psi[s, m, 1]]) for m in (g, g + 1)]))
        pairs = times_left(times_right(high, low, table_right), table_left)
        for real, imag in pairs:
            inten = inten + (real * real + imag * imag)
        far += pairs
    factor = amps[s] * lax.rsqrt(jnp.maximum(inten, 0.25))
    for m, (real, imag) in enumerate(far):
        far_high[s, m], far_low[s, m] = hilo(columns([real * factor, imag * factor]))


def backward(s, probe, table_right, table_left, patch, psi, far_high, far_low, sums):
    num_re, num_im = jnp.zeros((W, W), F32), jnp.zeros((W, W), F32)
    for g in range(0, probe.shape[0], 2):
        high, low = rows_of([far_high[s, g], far_high[s, g + 1]]), rows_of([far_low[s, g], far_low[s, g + 1]])
        pairs = times_left(times_right(high, low, table_right), table_left)
        for m, (real, imag) in zip((g, g + 1), pairs):
            chi_re, chi_im = real - psi[s, m, 0], imag - psi[s, m, 1]
            num_re = num_re + (probe[m, 0] * chi_re + probe[m, 1] * chi_im)
            num_im = num_im + (probe[m, 0] * chi_im - probe[m, 1] * chi_re)
            add_plane(sums, 2 * m, patch[s, 0] * chi_re + patch[s, 1] * chi_im)
            add_plane(sums, 2 * m + 1, patch[s, 0] * chi_im - patch[s, 1] * chi_re)
    return num_re, num_im


DEPTH = 8
PLANE_STEPS = sorted(
    ((dx, dy) for dx in range(4) for dy in range(4) if dx + dy > 0),
    key=lambda step: -(min(step[0], 4 - step[0]) + min(step[1], 4 - step[1])),
)
DEPTH_STEPS = sorted(range(1, DEPTH), key=lambda step: -min(step, DEPTH - step))
UNIT = W // 8
TILES = 10 * UNIT
HALF = TILES // 2
SHARE = HALF // PLANE


def add_plane(sums, plane, value):
    here = pl.ds(plane * UNIT, UNIT)
    sums[here] += value.reshape(UNIT, 8, W)


def placed(shifted, plane, place, count, acc, target):
    lane = lax.broadcasted_iota(jnp.int32, (W, W), 1)
    for part in range(3):

        def add(s, blocks):
            top, left, live = place(s)
            value = shifted[s, plane, pl.ds(2 * W + part * W - top, W), :]
            out = []
            for j, block in enumerate(blocks):
                at = lane + (j * W - left)
                inside = jnp.logical_and(at >= 0, at < live * W)
                out.append(block + jnp.where(inside, value, 0.0))
            return tuple(out)

        blocks = lax.fori_loop(0, count, add, tuple(jnp.zeros((W, W), F32) for _ in range(3)), unroll=True)
        for j in range(3):
            acc[target, j, pl.ds(part * W, W), :] = blocks[j]


def step_kernel(rows, cols, offsets_hbm, counts_hbm, *refs):
    (obj, *hbm), (updated, direction) = refs[:7], refs[7:9]
    (offsets, counts, patch, psi, far_high, far_low, shifted, acc, sums, got, gathered, shard, layers, total) = refs[9:23]
    (from_left, from_above, from_corner, from_high, relay, halo_relay) = refs[23:29]
    (load, halo_send, halo_recv, send, recv, ar_send, ar_recv, ext, *vmem) = refs[29:]
    probe, amps, right_fwd, right_inv, left_fwd, left_inv = vmem
    slot_count = amps.shape[0]
    r, c = position()
    core, z_lo = lax.rem(r, 2), r // 2
    z_hi, xy = c // PLANE, lax.rem(c, PLANE)
    z = z_hi * (DEPTH // 2) + z_lo
    left, up = c > 0, r > 0
    right, down = c < cols - 1, r < rows - 1
    up_left, down_right = jnp.logical_and(up, left), jnp.logical_and(down, right)
    near_right, near_left = jnp.logical_and(right, c != PLANE - 1), jnp.logical_and(left, c != PLANE)
    up_right, turning = jnp.logical_and(up, near_right), jnp.logical_and(down, near_right)
    source, target = c == PLANE - 1, c == PLANE
    target_up = jnp.logical_and(target, up)
    passing = [c == spot for spot in SUMS_RELAYS]
    passing = passing[:2] + [jnp.logical_and(flag, down) for flag in passing[2:]]
    sourced = [source] * 2 + [jnp.logical_and(source, down)] * 2
    east, south, southeast = (r, c + 1), (r + 1, c), (r + 1, c + 1)
    twin = (r + 1 - 2 * core, c)

    def in_plane(k):
        dx, dy = PLANE_STEPS[k - 1]
        other = lax.rem(xy // 4 + dx, 4) * 4 + lax.rem(xy + dy, 4)
        return other, (r, z_hi * PLANE + other)

    def in_depth(k):
        other = lax.rem(z + DEPTH_STEPS[k - 1], DEPTH)
        half = DEPTH // 2
        return lax.rem(other, half) * 2 + core, (other // half) * PLANE + xy

    pieces = [(obj.at[:, :, pl.ds(k * W, W)], ext.at[:, k, pl.ds(0, 2 * W)]) for k in range(2)]
    pieces += [(offsets_hbm, offsets), (counts_hbm, counts)]
    pieces += list(zip(hbm, vmem))
    copies = [pltpu.make_async_copy(src, dst, load.at[k]) for k, (src, dst) in enumerate(pieces)]
    for copy in copies:
        copy.start()

    barrier = pltpu.get_barrier_semaphore()
    peers = [twin] + [in_plane(k)[1] for k in range(1, PLANE)] + [in_depth(k) for k in range(1, DEPTH)]
    ahead = [c == PLANE + spot for spot in HALO_RELAYS]
    ahead_up = [jnp.logical_and(flag, up) for flag in ahead]
    target_down = jnp.logical_and(source, down)
    greetings = [(source, (r, PLANE + spot)) for spot in HALO_RELAYS]
    greetings += [(target_down, (r + 1, PLANE + spot)) for spot in HALO_RELAYS]
    for when, device in greetings:

        @pl.when(when)
        def _():
            pl.semaphore_signal(barrier, inc=1, device_id=device, device_id_type=MESH)

    for device in peers:
        pl.semaphore_signal(barrier, inc=1, device_id=device, device_id_type=MESH)
    greetings = []
    greetings += [(flag, (r, PLANE)) for flag in ahead] + [(near_right, east), (down, south)]
    waits = [near_left, up, *[target for _ in HALO_RELAYS], *ahead, *ahead_up]
    greetings += [(left, (r, c - 1)), (up, (r - 1, c)), (up_left, (r - 1, c - 1))]
    greetings += [(target, (r, spot)) for spot in SUMS_RELAYS[:2]]
    greetings += [(target_up, (r - 1, spot)) for spot in SUMS_RELAYS[2:]]
    greetings += [(flag, (r, PLANE - 1)) for flag in passing]
    for when, device in greetings:

        @pl.when(when)
        def _():
            pl.semaphore_signal(barrier, inc=1, device_id=device, device_id_type=MESH)

    waits += [right, down, down_right, *sourced, *passing]

    def place(s):
        return offsets[0, s], offsets[1, s], (s < counts[0, 0]).astype(jnp.int32)

    def remote(k, j, src, dst, device):
        return pltpu.make_async_remote_copy(src, dst, send.at[k], recv.at[j], device_id=device, device_id_type=MESH)

    def landed(when, ref, semaphore):
        wait = pltpu.make_async_copy(ref, ref, semaphore).wait
        if when is None:
            wait()
        else:
            pl.when(when)(wait)

    def summed(k, src, dst, device):
        return pltpu.make_async_remote_copy(src, dst, ar_send.at[k], ar_recv.at[k], device_id=device, device_id_type=MESH)

    def halo(k, j, src, dst, device):
        return pltpu.make_async_remote_copy(
            src, dst, halo_send.at[k], halo_recv.at[j], device_id=device, device_id_type=MESH
        )

    upper, lower, under_rows = pl.ds(0, W), pl.ds(W, W), pl.ds(2 * W, W)
    west, north = (r, c - 1), (r - 1, c)
    exchange = [
        (near_left, near_right, halo(0, 0, ext.at[:, 0, upper], ext.at[:, 2, upper], west)),
        (up, down, halo(1, 1, ext.at[:, 0, upper], ext.at[:, 0, under_rows], north)),
        (up, down, halo(2, 2, ext.at[:, 1, upper], ext.at[:, 1, under_rows], north)),
        (near_left, near_right, halo(3, 3, ext.at[:, 0, lower], ext.at[:, 2, lower], west)),
    ]
    handed = halo(4, 4, ext.at[:, 2, upper], ext.at[:, 2, under_rows], north)
    relays = len(HALO_RELAYS)
    share = 2 * W // relays
    there, back, above = [], [], []
    for half in range(2):
        for i, spot in enumerate(HALO_RELAYS):
            plane, start = i % 2, i // 2 * share
            span = pl.ds(half * W + start, share)
            held = halo_relay.at[half]
            there.append((target, ahead[i], halo(5, 5 + half, ext.at[plane, 0, span], held, (r, PLANE + spot))))
            back.append((ahead[i], source, halo(6 + half, 7 + half, held, ext.at[plane, 2, span], (r, PLANE - 1))))
            if half == 0:
                corner_rows = ext.at[plane, 2, pl.ds(2 * W + start, share)]
                above.append((ahead_up[i], target_down, halo(8, 9, held, corner_rows, (r - 1, PLANE - 1))))
    for copy in copies[:2]:
        copy.wait()
    pl.semaphore_wait(barrier, len(peers) + count(*waits))
    for sends, _, copy in there + exchange:
        pl.when(sends)(copy.start)
    for (_, flag, arriving), (_, _, leaving) in zip(there, back):

        @pl.when(flag)
        def _():
            arriving.wait_recv()
            leaving.start()

    for flag, _, copy in above:
        pl.when(flag)(copy.start)

    shifted[...] = jnp.zeros_like(shifted)
    sums[...] = jnp.zeros_like(sums)
    for copy in copies[2:]:
        copy.wait()

    power = jnp.zeros((W, W), F32)
    for m in range(probe.shape[0]):
        power = power + (probe[m, 0] * probe[m, 0] + probe[m, 1] * probe[m, 1])

    def weigh(s, carry):
        shifted[s, 2, pl.ds(2 * W, W), :] = pltpu.roll(power, place(s)[1] % W, 1)
        return carry

    lax.fori_loop(0, slot_count, weigh, 0, unroll=True)
    placed(shifted, 2, place, slot_count, acc, 2)
    strip, under, corner = acc.at[:, 2, pl.ds(0, 2 * W)], acc.at[:, pl.ds(0, 2), pl.ds(2 * W, W)], acc.at[:, 2, pl.ds(2 * W, W)]
    weights = [
        (right, left, remote(0, 0, strip.at[2], from_left.at[2], east)),
        (down, up, remote(1, 1, under.at[2], from_above.at[2], south)),
        (down_right, up_left, remote(2, 2, corner.at[2], from_corner.at[2], southeast)),
    ]
    for sends, _, copy in weights:
        pl.when(sends)(copy.start)

    pl.when(near_right)(exchange[0][2].wait_recv)
    pl.when(up_right)(handed.start)
    for _, receives, copy in exchange[1:] + [(up_right, turning, handed)]:
        pl.when(receives)(copy.wait_recv)
    landed(source, ext.at[:, 2, upper], halo_recv.at[7])
    landed(source, ext.at[:, 2, lower], halo_recv.at[8])
    landed(target_down, ext.at[:, 2, under_rows], halo_recv.at[9])

    def first(s, carry):
        forward(s, place(s), ext, probe, amps, right_fwd, left_fwd, patch, psi, far_high, far_low, sums)
        return carry

    lax.fori_loop(0, slot_count, first, 0, unroll=True)

    def second(s, carry):
        turn = place(s)[1] % W
        for plane, value in enumerate(backward(s, probe, right_inv, left_inv, patch, psi, far_high, far_low, sums)):
            shifted[s, plane, pl.ds(2 * W, W), :] = pltpu.roll(value, turn, 1)
        return carry

    lax.fori_loop(0, slot_count, second, 0, unroll=True)

    mine = pl.ds(core * HALF, HALF)
    swap = summed(0, sums.at[pl.ds((1 - core) * HALF, HALF)], got, twin)
    swap.start()
    placed(shifted, 0, place, slot_count, acc, 0)
    swap.wait_recv()
    got[...] += sums[mine]

    for k in range(1, PLANE):
        other, device = in_plane(k)
        summed(1, got.at[pl.ds(other * SHARE, SHARE)], gathered.at[k - 1], device).start()
    placed(shifted, 1, place, slot_count, acc, 1)
    numer = pl.ds(0, 2)
    crossing = [(strip.at[p, lower], from_left.at[p, lower], (r, PLANE)) for p in range(2)]
    crossing += [(corner.at[p], from_corner.at[p], (r + 1, PLANE)) for p in range(2)]
    pass_on = [remote(3 + i, 3, src, relay, (r, spot)) for i, ((src, _, _), spot) in enumerate(zip(crossing, SUMS_RELAYS))]
    passed = [remote(7, 4 + i // 2, relay, dst, device) for i, (_, dst, device) in enumerate(crossing)]
    turned = remote(8, 6, corner.at[numer], from_high, south)
    plan = [
        (turning, up_right, turned),
        (near_right, near_left, remote(9, 7, strip.at[numer, lower], from_left.at[numer, lower], east)),
        (down, up, remote(10, 8, under.at[numer], from_above.at[numer], south)),
    ]
    late = remote(11, 9, strip.at[numer, upper], from_left.at[numer, upper], east)
    for flag, copy in zip(sourced, pass_on):
        pl.when(flag)(copy.start)
    pl.when(source)(late.start)
    for sends, _, copy in plan:
        pl.when(sends)(copy.start)
    value = got[pl.ds(xy * SHARE, SHARE)]
    landed(None, gathered, ar_recv.at[1])
    for k in range(1, PLANE):
        value = value + gathered[k - 1]
    shard[...] = value

    for k in range(1, DEPTH):
        summed(2, shard, layers.at[z], in_depth(k)).start()
    layers[z] = value
    for flag, arriving, leaving in zip(passing, pass_on, passed):

        @pl.when(flag)
        def _():
            arriving.wait_recv()
            leaving.start()

    @pl.when(up_right)
    def _():
        turned.wait_recv()
        strip[numer, upper] += from_high[...]

    pl.when(near_right)(late.start)
    landed(None, layers.at[pl.ds(0, DEPTH - 1)], ar_recv.at[2])
    value = layers[0]
    for k in range(1, DEPTH):
        value = value + layers[k]
    here = pl.ds(core * HALF + xy * SHARE, SHARE)
    total[here] = value

    for k in range(1, PLANE):
        summed(3, total.at[here], total.at[here], in_plane(k)[1]).start()

    others = pl.ds(core * HALF, HALF - SHARE)
    landed(None, total.at[others], ar_recv.at[3])
    half = total.at[mine]
    last = summed(4, half, half, twin)
    last.start()

    for _, receives, copy in weights + plan[1:]:
        pl.when(receives)(copy.wait_recv)
    landed(target, from_left.at[numer, lower], recv.at[4])
    landed(target_up, from_corner.at[numer], recv.at[5])
    pl.when(left)(late.wait_recv)

    def taken(flag, value):
        return jnp.where(jnp.broadcast_to(flag.astype(jnp.int32), value.shape) > 0, value, 0.0)

    for i in range(2):
        for j in range(2):
            span = pl.ds(i * W, W)
            parts = []
            for plane in range(3):
                value = acc[plane, j, span, :]
                if j == 0:
                    value = value + taken(left, from_left[plane, span, :])
                if i == 0:
                    value = value + taken(up, from_above[plane, j])
                if i == 0 and j == 0:
                    value = value + taken(up_left if plane == 2 else target_up, from_corner[plane])
                parts.append(value)
            scale = 1.0 / (parts[2] + 1.0)
            for plane in range(2):
                updated[plane, span, pl.ds(j * W, W)] = ext[plane, j, span, :] + parts[plane] * scale

    last.wait_recv()
    scale = lax.rsqrt(total[pl.ds(8 * UNIT, UNIT)] + 1.0)
    for plane in range(8):
        direction[plane] = total[pl.ds(plane * UNIT, UNIT)] * scale
    for copy in [swap, last]:
        copy.wait_send()
    landed(None, got.at[pl.ds(0, HALF - SHARE)], ar_send.at[1])
    landed(None, layers.at[pl.ds(0, DEPTH - 1)], ar_send.at[2])
    landed(None, total.at[others], ar_send.at[3])
    for sends, _, copy in exchange + back + above + [(up_right, turning, handed)] + weights + plan:
        pl.when(sends)(copy.wait_send)
    landed(target, ext.at[:, 0, pl.ds(0, 2 * W)], halo_send.at[5])
    for flag, copy in zip(sourced + passing, pass_on + passed):
        pl.when(flag)(copy.wait_send)
    pl.when(right)(late.wait_send)


def step(obj, probe, offsets, counts, amps, rows, cols):
    fwd, inv = tables()
    consts = [
        np.concatenate([fwd[0], fwd[0], fwd[1]], 0),
        np.concatenate([inv[0], inv[0], inv[1]], 0),
        np.concatenate([inv[0], inv[1]], 0),
        np.concatenate([fwd[0], fwd[1]], 0),
    ]
    loaded = [probe, amps] + [jnp.asarray(v) for v in consts]
    slot_count, modes = amps.shape[0], probe.shape[0]
    dma = pltpu.SemaphoreType.DMA
    messages = 5
    return pl.pallas_call(
        functools.partial(step_kernel, rows, cols),
        out_shape=(
            pltpu.VMEM(obj.shape, F32),
            pltpu.VMEM((8, UNIT, 8, W), F32),
        ),
        in_specs=[HBM] * 9,
        out_specs=(VMEM, VMEM),
        scratch_shapes=[
            pltpu.SMEM(offsets.shape[::-1], jnp.int32),
            pltpu.SMEM((1, 1), jnp.int32),
            pltpu.VMEM((slot_count, 2, W, W), F32),
            pltpu.VMEM((slot_count, modes, 2, W, W), F32),
            pltpu.VMEM((slot_count, modes, W, 2 * W), BF),
            pltpu.VMEM((slot_count, modes, W, 2 * W), BF),
            pltpu.VMEM((slot_count, 3, 5 * W, W), F32),
            pltpu.VMEM((3, 3, 3 * W, W), F32),
            pltpu.VMEM((TILES, 8, W), F32),
            pltpu.VMEM((HALF, 8, W), F32),
            pltpu.VMEM((PLANE - 1, SHARE, 8, W), F32),
            pltpu.VMEM((SHARE, 8, W), F32),
            pltpu.VMEM((DEPTH, SHARE, 8, W), F32),
            pltpu.VMEM((TILES, 8, W), F32),
            pltpu.VMEM((3, 2 * W, W), F32),
            pltpu.VMEM((3, 2, W, W), F32),
            pltpu.VMEM((3, W, W), F32),
            pltpu.VMEM((2, W, W), F32),
            pltpu.VMEM((W, W), F32),
            pltpu.VMEM((2, 2 * W // len(HALO_RELAYS), W), F32),
            dma((10,)),
            dma((9,)),
            dma((10,)),
            dma((12,)),
            dma((10,)),
            dma((messages,)),
            dma((messages,)),
            pltpu.VMEM((2, 3, 3 * W, W), F32),
        ]
        + [pltpu.VMEM(v.shape, v.dtype) for v in loaded],
        compiler_params=pltpu.CompilerParams(collective_id=0, has_side_effects=True, vmem_limit_bytes=LIMIT),
        name="step",
    )(offsets.T, counts[None], obj, *loaded)


def finish_kernel(held_object, held_direction, new_object, direction, done):
    copies = [
        pltpu.make_async_copy(held_object, new_object, done.at[0]),
        pltpu.make_async_copy(held_direction, direction, done.at[1]),
    ]
    for copy in copies:
        copy.start()
    for copy in copies:
        copy.wait()


def finish(held_object, held_direction):
    return pl.pallas_call(
        finish_kernel,
        out_shape=(
            jax.ShapeDtypeStruct(held_object.shape, F32),
            jax.ShapeDtypeStruct(held_direction.shape, F32),
        ),
        in_specs=[VMEM, VMEM],
        out_specs=(HBM, HBM),
        scratch_shapes=[pltpu.SemaphoreType.DMA((2,))],
        compiler_params=pltpu.CompilerParams(vmem_limit_bytes=16 * 2**20),
        name="finish",
    )(held_object, held_direction)


def body(rows, cols, object_field, probe, offsets, counts, amplitudes):
    held = step(object_field, probe, offsets, counts, amplitudes, rows, cols)
    new_object, direction = finish(*held)
    return new_object, direction.reshape(probe.shape)


def solution(mesh):
    rows, cols = mesh.shape["row"], mesh.shape["col"]
    return jax.shard_map(
        functools.partial(body, rows, cols),
        mesh=mesh,
        in_specs=(
            P(None, "row", "col"),
            P(),
            P(("row", "col"), None),
            P(("row", "col")),
            P(("row", "col"), None, None),
        ),
        out_specs=(P(None, "row", "col"), P()),
        check_vma=False,
    )
```

```python
import functools

import jax
import jax.numpy as jnp
import ml_dtypes
import numpy as np
from jax import lax
from jax.experimental import pallas as pl
from jax.experimental.pallas import tpu as pltpu
from jax.sharding import PartitionSpec as P

BF = jnp.bfloat16
F32 = jnp.float32
W = 128
MESH = pl.DeviceIdType.MESH
HBM = pl.BlockSpec(memory_space=pl.ANY)
VMEM = pl.BlockSpec(memory_space=pltpu.VMEM)
SMEM = pl.BlockSpec(memory_space=pltpu.SMEM)
LIMIT = 56 * 2**20


def tables():
    index = np.arange(W)
    angle = (index[:, None] * index[None, :] % W) * (2 * np.pi / W)
    cosine, sine = np.cos(angle) / np.sqrt(W), np.sin(angle) / np.sqrt(W)

    def split(matrix):
        matrix = matrix.astype(np.float32)
        high = matrix.astype(ml_dtypes.bfloat16)
        return high, (matrix - high.astype(np.float32)).astype(ml_dtypes.bfloat16)

    fwd = split(np.block([[cosine, -sine], [sine, cosine]]))
    inv = split(np.block([[cosine, sine], [-sine, cosine]]))
    return fwd, inv


def position():
    return lax.axis_index("row"), lax.axis_index("col")


def count(*flags):
    return sum(flag.astype(jnp.int32) for flag in flags)


PLANE = 16
HALO_RELAYS = (12, 4, 1, 3, 15, 5, 13, 7)
SUMS_RELAYS = (0, 12, 13, 14)


def hilo(x):
    high = x.astype(BF)
    return high, (x - high.astype(F32)).astype(BF)


def dot(a, b):
    return jnp.dot(a, b, preferred_element_type=F32)


def columns(parts):
    return jnp.concatenate(parts, axis=1)


def rows_of(parts):
    return jnp.concatenate(parts, axis=0)


def times_right(high, low, table):
    out = dot(columns([high, low, high]), table[...])
    return [(out[k * W : (k + 1) * W, :W], out[k * W : (k + 1) * W, W:]) for k in range(2)]


def times_left(pairs, table):
    high, low = hilo(columns([rows_of(pair) for pair in pairs]))
    out = dot(table[...], high)
    out = out[: 2 * W] + out[2 * W :] + dot(table[: 2 * W], low)
    return [(out[:W, k * W : (k + 1) * W], out[W:, k * W : (k + 1) * W]) for k in range(2)]


def forward(s, place, ext, probe, amps, table_right, table_left, patch, psi, far_high, far_low, sums):
    top, left, live = place
    block, lanes = left // W, left % W
    lane = lax.broadcasted_iota(jnp.int32, (W, W), 1)
    kept = lane < live * W

    def cut(plane):
        first = ext[plane, block, pl.ds(top, W), :]
        second = ext[plane, block + 1, pl.ds(top, W), :]
        turned = pltpu.roll(jnp.where(lane >= lanes, first, second), (W - lanes) % W, 1)
        return jnp.where(kept, turned, 0.0)

    ore, oim = cut(0), cut(1)
    patch[s, 0], patch[s, 1] = ore, oim
    add_plane(sums, WEIGHT, ore * ore + oim * oim)
    inten = jnp.zeros((W, W), F32)
    far = []
    for g in range(0, probe.shape[0], 2):
        for m in (g, g + 1):
            psi[s, m, 0] = probe[m, 0] * ore - probe[m, 1] * oim
            psi[s, m, 1] = probe[m, 0] * oim + probe[m, 1] * ore
        high, low = hilo(rows_of([columns([psi[s, m, 0], psi[s, m, 1]]) for m in (g, g + 1)]))
        pairs = times_left(times_right(high, low, table_right), table_left)
        for real, imag in pairs:
            inten = inten + (real * real + imag * imag)
        far += pairs
    factor = amps[s] * lax.rsqrt(jnp.maximum(inten, 0.25))
    for m, (real, imag) in enumerate(far):
        far_high[s, m], far_low[s, m] = hilo(columns([real * factor, imag * factor]))


def backward(s, g, probe, table_right, table_left, patch, psi, far_high, far_low, sums):
    num_re, num_im = jnp.zeros((W, W), F32), jnp.zeros((W, W), F32)
    high, low = rows_of([far_high[s, g], far_high[s, g + 1]]), rows_of([far_low[s, g], far_low[s, g + 1]])
    pairs = times_left(times_right(high, low, table_right), table_left)
    for m, (real, imag) in zip((g, g + 1), pairs):
        chi_re, chi_im = real - psi[s, m, 0], imag - psi[s, m, 1]
        num_re = num_re + (probe[m, 0] * chi_re + probe[m, 1] * chi_im)
        num_im = num_im + (probe[m, 0] * chi_im - probe[m, 1] * chi_re)
        add_plane(sums, MODE_PLANES[2 * m], patch[s, 0] * chi_re + patch[s, 1] * chi_im)
        add_plane(sums, MODE_PLANES[2 * m + 1], patch[s, 0] * chi_im - patch[s, 1] * chi_re)
    return num_re, num_im


DEPTH = 8
PLANE_STEPS = sorted(
    ((dx, dy) for dx in range(4) for dy in range(4) if dx + dy > 0),
    key=lambda step: -(min(step[0], 4 - step[0]) + min(step[1], 4 - step[1])),
)
DEPTH_STEPS = sorted(range(1, DEPTH), key=lambda step: -min(step, DEPTH - step))
UNIT = W // 8
TILES = 10 * UNIT
HALF = TILES // 2
SHARE = HALF // PLANE
MODE_PLANES, WEIGHT = (0, 1, 2, 3, 5, 6, 7, 8), 4


def add_plane(sums, plane, value):
    here = pl.ds(plane * UNIT, UNIT)
    sums[here] += value.reshape(UNIT, 8, W)


def placed(shifted, plane, place, count, acc, target):
    lane = lax.broadcasted_iota(jnp.int32, (W, W), 1)
    for part in range(3):

        def add(s, blocks):
            top, left, live = place(s)
            value = shifted[s, plane, pl.ds(2 * W + part * W - top, W), :]
            out = []
            for j, block in enumerate(blocks):
                at = lane + (j * W - left)
                inside = jnp.logical_and(at >= 0, at < live * W)
                out.append(block + jnp.where(inside, value, 0.0))
            return tuple(out)

        blocks = lax.fori_loop(0, count, add, tuple(jnp.zeros((W, W), F32) for _ in range(3)), unroll=True)
        for j in range(3):
            acc[target, j, pl.ds(part * W, W), :] = blocks[j]


def step_kernel(rows, cols, offsets_hbm, counts_hbm, *refs):
    (obj, *hbm), (updated, direction) = refs[:7], refs[7:9]
    (offsets, counts, patch, psi, far_high, far_low, shifted, acc, sums, got, gathered, shard, layers, total) = refs[9:23]
    (from_left, from_above, from_corner, from_high, relay, halo_relay) = refs[23:29]
    (load, halo_send, halo_recv, send, recv, ar_send, ar_recv, ext, *vmem) = refs[29:]
    probe, amps, right_fwd, right_inv, left_fwd, left_inv = vmem
    slot_count = amps.shape[0]
    r, c = position()
    core, z_lo = lax.rem(r, 2), r // 2
    z_hi, xy = c // PLANE, lax.rem(c, PLANE)
    z = z_hi * (DEPTH // 2) + z_lo
    left, up = c > 0, r > 0
    right, down = c < cols - 1, r < rows - 1
    up_left, down_right = jnp.logical_and(up, left), jnp.logical_and(down, right)
    near_right, near_left = jnp.logical_and(right, c != PLANE - 1), jnp.logical_and(left, c != PLANE)
    up_right, turning = jnp.logical_and(up, near_right), jnp.logical_and(down, near_right)
    source, target = c == PLANE - 1, c == PLANE
    target_up = jnp.logical_and(target, up)
    passing = [c == spot for spot in SUMS_RELAYS]
    passing = passing[:2] + [jnp.logical_and(flag, down) for flag in passing[2:]]
    sourced = [source] * 2 + [jnp.logical_and(source, down)] * 2
    east, south, southeast = (r, c + 1), (r + 1, c), (r + 1, c + 1)
    twin = (r + 1 - 2 * core, c)

    def in_plane(k):
        dx, dy = PLANE_STEPS[k - 1]
        other = lax.rem(xy // 4 + dx, 4) * 4 + lax.rem(xy + dy, 4)
        return other, (r, z_hi * PLANE + other)

    def in_depth(k):
        other = lax.rem(z + DEPTH_STEPS[k - 1], DEPTH)
        half = DEPTH // 2
        return lax.rem(other, half) * 2 + core, (other // half) * PLANE + xy

    pieces = [(obj.at[:, :, pl.ds(k * W, W)], ext.at[:, k, pl.ds(0, 2 * W)]) for k in range(2)]
    pieces += [(offsets_hbm, offsets), (counts_hbm, counts)]
    pieces += list(zip(hbm, vmem))
    copies = [pltpu.make_async_copy(src, dst, load.at[k]) for k, (src, dst) in enumerate(pieces)]
    for copy in copies:
        copy.start()

    barrier = pltpu.get_barrier_semaphore()
    peers = [twin] + [in_plane(k)[1] for k in range(1, PLANE)] + [in_depth(k) for k in range(1, DEPTH)]
    ahead = [c == PLANE + spot for spot in HALO_RELAYS]
    ahead_up = [jnp.logical_and(flag, up) for flag in ahead]
    target_down = jnp.logical_and(source, down)
    greetings = [(source, (r, PLANE + spot)) for spot in HALO_RELAYS]
    greetings += [(target_down, (r + 1, PLANE + spot)) for spot in HALO_RELAYS]
    greetings += [(flag, (r, PLANE)) for flag in ahead] + [(near_right, east), (down, south)]
    waits = [near_left, up, *[target for _ in HALO_RELAYS], *ahead, *ahead_up]
    greetings += [(left, (r, c - 1)), (up, (r - 1, c)), (up_left, (r - 1, c - 1))]
    greetings += [(target, (r, spot)) for spot in SUMS_RELAYS[:2]]
    greetings += [(target_up, (r - 1, spot)) for spot in SUMS_RELAYS[2:]]
    greetings += [(flag, (r, PLANE - 1)) for flag in passing]
    for when, device in greetings:

        @pl.when(when)
        def _():
            pl.semaphore_signal(barrier, inc=1, device_id=device, device_id_type=MESH)

    for device in peers:
        pl.semaphore_signal(barrier, inc=1, device_id=device, device_id_type=MESH)
    waits += [right, down, down_right, *sourced, *passing]

    def place(s):
        return offsets[0, s], offsets[1, s], (s < counts[0, 0]).astype(jnp.int32)

    def remote(k, j, src, dst, device):
        return pltpu.make_async_remote_copy(src, dst, send.at[k], recv.at[j], device_id=device, device_id_type=MESH)

    def landed(when, ref, semaphore):
        wait = pltpu.make_async_copy(ref, ref, semaphore).wait
        if when is None:
            wait()
        else:
            pl.when(when)(wait)

    def summed(k, src, dst, device):
        return pltpu.make_async_remote_copy(src, dst, ar_send.at[k], ar_recv.at[k], device_id=device, device_id_type=MESH)

    def halo(k, j, src, dst, device):
        return pltpu.make_async_remote_copy(
            src, dst, halo_send.at[k], halo_recv.at[j], device_id=device, device_id_type=MESH
        )

    upper, lower, under_rows = pl.ds(0, W), pl.ds(W, W), pl.ds(2 * W, W)
    west, north = (r, c - 1), (r - 1, c)
    exchange = [
        (near_left, near_right, halo(0, 0, ext.at[:, 0, upper], ext.at[:, 2, upper], west)),
        (up, down, halo(1, 1, ext.at[:, 0, upper], ext.at[:, 0, under_rows], north)),
        (up, down, halo(2, 2, ext.at[:, 1, upper], ext.at[:, 1, under_rows], north)),
        (near_left, near_right, halo(3, 3, ext.at[:, 0, lower], ext.at[:, 2, lower], west)),
    ]
    handed = halo(4, 4, ext.at[:, 2, upper], ext.at[:, 2, under_rows], north)
    relays = len(HALO_RELAYS)
    share = 2 * W // relays
    there, back, above = [], [], []
    for half in range(2):
        for i, spot in enumerate(HALO_RELAYS):
            plane, start = i % 2, i // 2 * share
            span = pl.ds(half * W + start, share)
            held = halo_relay.at[half]
            there.append((target, ahead[i], halo(5, 5 + half, ext.at[plane, 0, span], held, (r, PLANE + spot))))
            back.append((ahead[i], source, halo(6 + half, 7 + half, held, ext.at[plane, 2, span], (r, PLANE - 1))))
            if half == 0:
                corner_rows = ext.at[plane, 2, pl.ds(2 * W + start, share)]
                above.append((ahead_up[i], target_down, halo(8, 9, held, corner_rows, (r - 1, PLANE - 1))))
    for copy in copies[:2]:
        copy.wait()
    pl.semaphore_wait(barrier, len(peers) + count(*waits))
    for sends, _, copy in there + exchange:
        pl.when(sends)(copy.start)

    shifted[...] = jnp.zeros_like(shifted)
    sums[...] = jnp.zeros_like(sums)
    for copy in copies[2:]:
        copy.wait()

    power = jnp.zeros((W, W), F32)
    for m in range(probe.shape[0]):
        power = power + (probe[m, 0] * probe[m, 0] + probe[m, 1] * probe[m, 1])

    def weigh(s, carry):
        shifted[s, 2, pl.ds(2 * W, W), :] = pltpu.roll(power, place(s)[1] % W, 1)
        return carry

    lax.fori_loop(0, slot_count, weigh, 0, unroll=True)
    placed(shifted, 2, place, slot_count, acc, 2)
    strip, under, corner = acc.at[:, 2, pl.ds(0, 2 * W)], acc.at[:, pl.ds(0, 2), pl.ds(2 * W, W)], acc.at[:, 2, pl.ds(2 * W, W)]
    weights = [
        (right, left, remote(0, 0, strip.at[2], from_left.at[2], east)),
        (down, up, remote(1, 1, under.at[2], from_above.at[2], south)),
        (down_right, up_left, remote(2, 2, corner.at[2], from_corner.at[2], southeast)),
    ]
    for sends, _, copy in weights:
        pl.when(sends)(copy.start)

    for (_, flag, arriving), (_, _, leaving) in zip(there, back):

        @pl.when(flag)
        def _():
            arriving.wait_recv()
            leaving.start()

    for flag, _, copy in above:
        pl.when(flag)(copy.start)
    pl.when(near_right)(exchange[0][2].wait_recv)
    pl.when(up_right)(handed.start)
    for _, receives, copy in exchange[1:] + [(up_right, turning, handed)]:
        pl.when(receives)(copy.wait_recv)
    landed(source, ext.at[:, 2, upper], halo_recv.at[7])
    landed(source, ext.at[:, 2, lower], halo_recv.at[8])
    landed(target_down, ext.at[:, 2, under_rows], halo_recv.at[9])

    def first(s, carry):
        forward(s, place(s), ext, probe, amps, right_fwd, left_fwd, patch, psi, far_high, far_low, sums)
        return carry

    lax.fori_loop(0, slot_count, first, 0, unroll=True)

    def second(g, s, carry):
        turn = place(s)[1] % W
        here = pl.ds(2 * W, W)
        for plane, value in enumerate(backward(s, g, probe, right_inv, left_inv, patch, psi, far_high, far_low, sums)):
            value = pltpu.roll(value, turn, 1)
            shifted[s, plane, here, :] = value if g == 0 else shifted[s, plane, here, :] + value
        return carry

    mine = pl.ds(core * HALF, HALF)
    swap = summed(0, sums.at[pl.ds((1 - core) * HALF, HALF)], got, twin)
    lax.fori_loop(0, slot_count, functools.partial(second, 0), 0, unroll=True)
    pl.when(core == 1)(swap.start)
    lax.fori_loop(0, slot_count, functools.partial(second, 2), 0, unroll=True)
    pl.when(core == 0)(swap.start)
    placed(shifted, 0, place, slot_count, acc, 0)
    swap.wait_recv()
    got[...] += sums[mine]

    for k in range(1, PLANE):
        other, device = in_plane(k)
        summed(1, got.at[pl.ds(other * SHARE, SHARE)], gathered.at[k - 1], device).start()
    placed(shifted, 1, place, slot_count, acc, 1)
    numer = pl.ds(0, 2)
    crossing = [(strip.at[p, lower], from_left.at[p, lower], (r, PLANE)) for p in range(2)]
    crossing += [(corner.at[p], from_corner.at[p], (r + 1, PLANE)) for p in range(2)]
    pass_on = [remote(3 + i, 3, src, relay, (r, spot)) for i, ((src, _, _), spot) in enumerate(zip(crossing, SUMS_RELAYS))]
    passed = [remote(7, 4 + i // 2, relay, dst, device) for i, (_, dst, device) in enumerate(crossing)]
    turned = remote(8, 6, corner.at[numer], from_high, south)
    plan = [
        (turning, up_right, turned),
        (near_right, near_left, remote(9, 7, strip.at[numer, lower], from_left.at[numer, lower], east)),
        (down, up, remote(10, 8, under.at[numer], from_above.at[numer], south)),
    ]
    late = remote(11, 9, strip.at[numer, upper], from_left.at[numer, upper], east)
    for flag, copy in zip(sourced, pass_on):
        pl.when(flag)(copy.start)
    pl.when(source)(late.start)
    for sends, _, copy in plan:
        pl.when(sends)(copy.start)
    value = got[pl.ds(xy * SHARE, SHARE)]
    landed(None, gathered, ar_recv.at[1])
    for k in range(1, PLANE):
        value = value + gathered[k - 1]
    shard[...] = value

    for k in range(1, DEPTH):
        summed(2, shard, layers.at[z], in_depth(k)).start()
    layers[z] = value
    for flag, arriving, leaving in zip(passing, pass_on, passed):

        @pl.when(flag)
        def _():
            arriving.wait_recv()
            leaving.start()

    @pl.when(up_right)
    def _():
        turned.wait_recv()
        strip[numer, upper] += from_high[...]

    pl.when(near_right)(late.start)
    landed(None, layers.at[pl.ds(0, DEPTH - 1)], ar_recv.at[2])
    value = layers[0]
    for k in range(1, DEPTH):
        value = value + layers[k]
    here = pl.ds(core * HALF + xy * SHARE, SHARE)
    total[here] = value

    for k in range(1, PLANE):
        summed(3, total.at[here], total.at[here], in_plane(k)[1]).start()

    others = pl.ds(core * HALF, HALF - SHARE)
    landed(None, total.at[others], ar_recv.at[3])
    half = total.at[mine]
    last = summed(4, half, half, twin)
    last.start()

    for _, receives, copy in weights + plan[1:]:
        pl.when(receives)(copy.wait_recv)
    landed(target, from_left.at[numer, lower], recv.at[4])
    landed(target_up, from_corner.at[numer], recv.at[5])
    pl.when(left)(late.wait_recv)

    def taken(flag, value):
        return jnp.where(jnp.broadcast_to(flag.astype(jnp.int32), value.shape) > 0, value, 0.0)

    for i in range(2):
        for j in range(2):
            span = pl.ds(i * W, W)
            parts = []
            for plane in range(3):
                value = acc[plane, j, span, :]
                if j == 0:
                    value = value + taken(left, from_left[plane, span, :])
                if i == 0:
                    value = value + taken(up, from_above[plane, j])
                if i == 0 and j == 0:
                    value = value + taken(up_left if plane == 2 else target_up, from_corner[plane])
                parts.append(value)
            scale = 1.0 / (parts[2] + 1.0)
            for plane in range(2):
                updated[plane, span, pl.ds(j * W, W)] = ext[plane, j, span, :] + parts[plane] * scale

    last.wait_recv()
    scale = lax.rsqrt(total[pl.ds(WEIGHT * UNIT, UNIT)] + 1.0)
    for k, plane in enumerate(MODE_PLANES):
        direction[k] = total[pl.ds(plane * UNIT, UNIT)] * scale
    for copy in [swap, last]:
        copy.wait_send()
    landed(None, got.at[pl.ds(0, HALF - SHARE)], ar_send.at[1])
    landed(None, layers.at[pl.ds(0, DEPTH - 1)], ar_send.at[2])
    landed(None, total.at[others], ar_send.at[3])
    for sends, _, copy in exchange + back + above + [(up_right, turning, handed)] + weights + plan:
        pl.when(sends)(copy.wait_send)
    landed(target, ext.at[:, 0, pl.ds(0, 2 * W)], halo_send.at[5])
    for flag, copy in zip(sourced + passing, pass_on + passed):
        pl.when(flag)(copy.wait_send)
    pl.when(right)(late.wait_send)


def step(obj, probe, offsets, counts, amps, rows, cols):
    fwd, inv = tables()
    consts = [
        np.concatenate([fwd[0], fwd[0], fwd[1]], 0),
        np.concatenate([inv[0], inv[0], inv[1]], 0),
        np.concatenate([inv[0], inv[1]], 0),
        np.concatenate([fwd[0], fwd[1]], 0),
    ]
    loaded = [probe, amps] + [jnp.asarray(v) for v in consts]
    slot_count, modes = amps.shape[0], probe.shape[0]
    dma = pltpu.SemaphoreType.DMA
    messages = 5
    return pl.pallas_call(
        functools.partial(step_kernel, rows, cols),
        out_shape=(
            pltpu.VMEM(obj.shape, F32),
            pltpu.VMEM((8, UNIT, 8, W), F32),
        ),
        in_specs=[HBM] * 9,
        out_specs=(VMEM, VMEM),
        scratch_shapes=[
            pltpu.SMEM(offsets.shape[::-1], jnp.int32),
            pltpu.SMEM((1, 1), jnp.int32),
            pltpu.VMEM((slot_count, 2, W, W), F32),
            pltpu.VMEM((slot_count, modes, 2, W, W), F32),
            pltpu.VMEM((slot_count, modes, W, 2 * W), BF),
            pltpu.VMEM((slot_count, modes, W, 2 * W), BF),
            pltpu.VMEM((slot_count, 3, 5 * W, W), F32),
            pltpu.VMEM((3, 3, 3 * W, W), F32),
            pltpu.VMEM((TILES, 8, W), F32),
            pltpu.VMEM((HALF, 8, W), F32),
            pltpu.VMEM((PLANE - 1, SHARE, 8, W), F32),
            pltpu.VMEM((SHARE, 8, W), F32),
            pltpu.VMEM((DEPTH, SHARE, 8, W), F32),
            pltpu.VMEM((TILES, 8, W), F32),
            pltpu.VMEM((3, 2 * W, W), F32),
            pltpu.VMEM((3, 2, W, W), F32),
            pltpu.VMEM((3, W, W), F32),
            pltpu.VMEM((2, W, W), F32),
            pltpu.VMEM((W, W), F32),
            pltpu.VMEM((2, 2 * W // len(HALO_RELAYS), W), F32),
            dma((10,)),
            dma((9,)),
            dma((10,)),
            dma((12,)),
            dma((10,)),
            dma((messages,)),
            dma((messages,)),
            pltpu.VMEM((2, 3, 3 * W, W), F32),
        ]
        + [pltpu.VMEM(v.shape, v.dtype) for v in loaded],
        compiler_params=pltpu.CompilerParams(collective_id=0, has_side_effects=True, vmem_limit_bytes=LIMIT),
        name="step",
    )(offsets.T, counts[None], obj, *loaded)


def finish_kernel(held_object, held_direction, new_object, direction, done):
    copies = [
        pltpu.make_async_copy(held_object, new_object, done.at[0]),
        pltpu.make_async_copy(held_direction, direction, done.at[1]),
    ]
    for copy in copies:
        copy.start()
    for copy in copies:
        copy.wait()


def finish(held_object, held_direction):
    return pl.pallas_call(
        finish_kernel,
        out_shape=(
            jax.ShapeDtypeStruct(held_object.shape, F32),
            jax.ShapeDtypeStruct(held_direction.shape, F32),
        ),
        in_specs=[VMEM, VMEM],
        out_specs=(HBM, HBM),
        scratch_shapes=[pltpu.SemaphoreType.DMA((2,))],
        compiler_params=pltpu.CompilerParams(vmem_limit_bytes=16 * 2**20),
        name="finish",
    )(held_object, held_direction)


def body(rows, cols, object_field, probe, offsets, counts, amplitudes):
    held = step(object_field, probe, offsets, counts, amplitudes, rows, cols)
    new_object, direction = finish(*held)
    return new_object, direction.reshape(probe.shape)


def solution(mesh):
    rows, cols = mesh.shape["row"], mesh.shape["col"]
    return jax.shard_map(
        functools.partial(body, rows, cols),
        mesh=mesh,
        in_specs=(
            P(None, "row", "col"),
            P(),
            P(("row", "col"), None),
            P(("row", "col")),
            P(("row", "col"), None, None),
        ),
        out_specs=(P(None, "row", "col"), P()),
        check_vma=False,
    )
```
